256 devices in a mesh: orb: 64 (over y_hi, x, z), grid: 4 (over y_lo, core).
Axes of the slice: x: 4, y: 4 (y_hi: 2, y_lo: 2; y = y_hi * 2 + y_lo), z: 8, core: 2. Of those that a mesh axis runs over, the one named last changes fastest.
Arguments:
- orbitals: float32 [64, 373248], P('orb', 'grid'), may hold values from -12 to 12
Outputs:
- residual: float32 [64, 373248], P('orb', 'grid')
- intersection: float32 [64, 1, 1], P('orb')
The draws below stay inside these ranges and needn't reach their ends.
All inputs are finite; a program needn't handle non-finite values.
Results may differ from the reference program's by a relative error of at most 0.00023.
Values sent between devices are 32-bit elements; how exact they have to be, the bound alone decides.
No kernel may reach another device: no remote copies, remote signals or barrier semaphores. Data moves between devices by JAX's collectives and lax.ppermute only.
A program may use at most 64 MiB of HBM per device.

```python
import math
import jax
import jax.numpy as jnp
from jax import lax

G = 72
ORB_DEV = 1
REACH = 4
BLOCKS = 64
N_ORBS = 64


def draw_orbitals(key, part):
    key = jax.random.fold_in(key, 7)
    subkeys = jax.random.split(key, 6)
    cell_index = jnp.arange(G * G * G, dtype=jnp.int32)
    xcoord = (cell_index // (G * G)).astype(jnp.float32)
    ycoord = (cell_index // G % G).astype(jnp.float32)
    zcoord = (cell_index % G).astype(jnp.float32)
    cell_scale = jnp.exp(jax.random.uniform(subkeys[1], (G * G * G,), jnp.float32, 0.0, math.log(3.2)))
    magnitudes = jax.random.uniform(subkeys[2], (N_ORBS, 3), jnp.float32, 0.3, 0.9)
    signs = jnp.where(jax.random.bernoulli(subkeys[3], 0.5, (N_ORBS, 3)), 1.0, -1.0)
    amplitudes = magnitudes * signs
    vectors = jax.random.randint(subkeys[4], (N_ORBS, 3, 3), -1, 2).astype(jnp.float32)
    phases = jax.random.uniform(subkeys[5], (N_ORBS, 3), jnp.float32, -math.pi, math.pi)
    smooth = jnp.zeros((N_ORBS, G * G * G), jnp.float32)
    for which in range(3):
        argument = (vectors[:, which, 0:1] * xcoord[None, :] + vectors[:, which, 1:2] * ycoord[None, :] + vectors[:, which, 2:3] * zcoord[None, :]) * (2.0 * math.pi / G) + phases[:, which:which + 1]
        smooth = smooth + amplitudes[:, which:which + 1] * jnp.cos(argument)
    rough = 0.6 * jax.random.truncated_normal(subkeys[0], -4.0, 4.0, (N_ORBS, G * G * G), jnp.float32)
    rise = 0.3
    envelope = jnp.exp(rise * xcoord / G)
    values = (rough + smooth) * (cell_scale * envelope)[None, :] * 0.5
    return jnp.clip(values, -12.0, 12.0)


def setup_inputs(seed: int = 0) -> dict:
    splits = jax.random.split(jax.random.key(seed), 2)
    orbitals = draw_orbitals(jax.random.fold_in(splits[1], 71), 0)
    return dict(orbitals=orbitals)


SCREENING = 0.09
FRACTION = 0.25


def wavenumber(indices, length):
    return jnp.minimum(indices, length - indices).astype(jnp.float32) * (2.0 * math.pi / length)


def screened(first, second, third):
    squared = first[:, None, None] ** 2 + second[None, :, None] ** 2 + third[None, None, :] ** 2
    scaled = squared / (4.0 * SCREENING * SCREENING)
    guarded = jnp.where(scaled > 0, scaled, 1.0)
    return jnp.where(scaled > 0, (1.0 - jnp.exp(-guarded)) / guarded, 1.0)


def screened_solve(density, kernel):
    spectrum = jnp.fft.rfftn(density, axes=(-3, -2, -1))
    return jnp.fft.irfftn(spectrum * kernel, s=(G, G, G), axes=(-3, -2, -1))


def pair_terms(target, source, kernel):
    density = target[:, None] * source[None, :]
    potential = screened_solve(density, kernel)
    own_share = jnp.sum(potential * source[None], axis=1)
    other_share = jnp.sum(potential * target[:, None], axis=0)
    return own_share, other_share


def reference(orbitals):
    indices = jnp.arange(G, dtype=jnp.int32)
    half_indices = jnp.arange(G // 2 + 1, dtype=jnp.int32)
    kernel = screened(wavenumber(indices, G), wavenumber(indices, G), wavenumber(half_indices, G))
    orbital_blocks = orbitals.reshape(BLOCKS, ORB_DEV, G, G, G)
    exchange = lax.map(lambda member: pair_terms(member, member, kernel)[0], orbital_blocks)
    for offset in range(1, REACH + 1):
        shifted = jnp.roll(orbital_blocks, offset, axis=0)
        own_share, other_share = lax.map(lambda paired: pair_terms(paired[0], paired[1], kernel), (orbital_blocks, shifted))
        exchange = exchange + own_share + jnp.roll(other_share, -offset, axis=0)
    exchange = -FRACTION * exchange.reshape(BLOCKS, ORB_DEV, G * G * G)
    flat_blocks = orbital_blocks.reshape(BLOCKS, ORB_DEV, G * G * G)
    intersection = jnp.einsum('oac,obc->oab', flat_blocks, exchange, precision=lax.Precision.HIGHEST) / float(G * G * G)
    residual = exchange - jnp.einsum('oab,oac->obc', intersection, flat_blocks, precision=lax.Precision.HIGHEST)
    return residual.reshape(N_ORBS, G * G * G), intersection
```

```python
import math

import jax
import jax.numpy as jnp
import numpy as np
from jax import lax
from jax.experimental import pallas as pl
from jax.experimental.pallas import tpu as pltpu
from jax.sharding import PartitionSpec as P

G = 72
LANES = 128
DEVICES = 4
STEPS = (0, 2, 3, 1)
PLANES = G // DEVICES
LINES = PLANES * G
ROWS = LINES * G // LANES
PAD_ROWS = 736
GROUPS = ROWS // 9
TILES = 11
PAIR_ROWS = 200
STEP = 24
SCREENING = 0.09
FRACTION = 0.25
CELLS = float(G * G * G)


def hartley_halves():
    indices = np.arange(G)
    phases = 2.0 * np.pi * (indices[:, None] * indices[None, :] % G) / G
    table = np.cos(phases) + np.sin(phases)
    high = table.astype(jnp.bfloat16)
    low = (table - high.astype(np.float64)).astype(jnp.bfloat16)
    return high, low


def line_weights():
    high, low = hartley_halves()
    weights = np.zeros((2 * LANES, 2 * LANES), jnp.bfloat16)
    weights[:G, :G] = high
    weights[:G, LANES : LANES + G] = low
    weights[LANES : LANES + G, :G] = high
    return weights


def column_weights():
    return np.concatenate(hartley_halves(), axis=0)


def spread(table):
    wide = np.zeros((G, DEVICES * STEP), jnp.bfloat16)
    for device in range(DEVICES):
        wide[:, device * STEP : device * STEP + PLANES] = table[:, device * PLANES : (device + 1) * PLANES]
    return wide


def in_order(table, device):
    blocks = np.split(table, DEVICES, axis=1)
    return np.concatenate([blocks[device ^ step] for step in STEPS], axis=1)


def forward_weights(device):
    return np.concatenate([spread(in_order(half, device)) for half in hartley_halves()], axis=0)


def backward_weights(device):
    return np.concatenate([spread(in_order(half, device)).T for half in hartley_halves()], axis=0)


def wavenumber(indices):
    return jnp.minimum(indices, G - indices).astype(jnp.float32) * (2.0 * math.pi / G)


def screened(device):
    lanes = jnp.arange(TILES * LANES, dtype=jnp.int32)
    first = wavenumber(jnp.arange(G, dtype=jnp.int32))
    second = wavenumber(jnp.minimum(device * PLANES + lanes // G, G - 1))
    third = wavenumber(lanes % G)
    squared = first[:, None] ** 2 + (second**2)[None, :] + (third**2)[None, :]
    scaled = squared / (4.0 * SCREENING * SCREENING)
    guarded = jnp.where(scaled > 0, scaled, 1.0)
    return jnp.where(scaled > 0, (1.0 - jnp.exp(-guarded)) / guarded, 1.0) / CELLS


def halves(value):
    high = value.astype(jnp.bfloat16)
    return high, (value - high.astype(jnp.float32)).astype(jnp.bfloat16)


def product(left, right):
    return jnp.dot(left, right, preferred_element_type=jnp.float32)


def along_lines(value, weights):
    result = product(jnp.concatenate(halves(value), axis=1), weights)
    return result[:, :LANES] + result[:, LANES:]


def along_columns(values, weights):
    rows = weights.shape[0] // 2
    high, low = halves(jnp.concatenate(values, axis=1) if len(values) > 1 else values[0])
    result = product(weights, high)
    result = result[:rows] + result[rows:] + product(weights[:rows], low)
    return [result[:, index * LANES : (index + 1) * LANES] for index in range(len(values))]


def unpack(lines, load, store, lane):
    tiles = {}

    def tile_at(tile):
        if tile not in tiles:
            tiles.pop(tile - 2, None)
            tiles[tile] = load(tile)
        return tiles[tile]

    for line in range(lines):
        tile, shift = divmod(line * G, LANES)
        value = tile_at(tile)
        if shift:
            value = pltpu.roll(value, LANES - shift, 1)
        if shift + G > LANES:
            tail = pltpu.roll(tile_at(tile + 1), LANES - shift, 1)
            value = jnp.where(lane < LANES - shift, value, tail)
        store(line, jnp.where(lane < G, value, 0.0))


def pack(lines, load, store, lane):
    filled = jnp.zeros(lane.shape, jnp.float32)
    for line in range(lines):
        tile, shift = divmod(line * G, LANES)
        value = load(line)
        if shift:
            value = pltpu.roll(value, shift, 1)
        if shift + G < LANES:
            filled = filled + value
            if line == lines - 1:
                store(tile, filled)
            continue
        store(tile, filled + jnp.where(lane >= shift, value, 0.0))
        filled = jnp.where(lane < shift, value, 0.0)
        if line == lines - 1 and shift + G > LANES:
            store(tile + 1, filled)


def lane_index(rows):
    return lax.broadcasted_iota(jnp.int32, (rows, LANES), 1)


def line_passes(work, weights, count):
    rows = 6 * G

    def some_lines(index, carry):
        block = pl.ds(pl.multiple_of(index * rows, 8), rows)
        work[block, :] = along_lines(work[block, :], weights[...])
        return carry

    lax.fori_loop(0, count * LINES // rows, some_lines, 0, unroll=True)


def column_passes(work, weights, count):
    def planes(index, carry):
        blocks = [pl.ds(pl.multiple_of((2 * index + half) * G, 8), G) for half in range(2)]
        values = along_columns([work[block, :] for block in blocks], weights[...])
        for block, value in zip(blocks, values):
            work[block, :] = value
        return carry

    lax.fori_loop(0, count * PLANES // 2, planes, 0, unroll=3)


def device_row(chunks, place, device, row):
    value = chunks[0][row : row + 1, :]
    for chunk, step in zip(chunks[1:], STEPS[1:]):
        value = jnp.where(place[1] ^ step == device, chunk[row : row + 1, :], value)
    return value


def orbital_at(refs, names, place, rows):
    def read(distance):
        if distance in names:
            return refs[names.index(distance)][rows, :]
        step = abs(distance)
        first = refs[names.index((step, 0))][rows, :]
        second = refs[names.index((step, 1))][rows, :]
        upward = place[0] == (0 if step == 1 else 1)
        return jnp.where(upward if distance > 0 else jnp.logical_not(upward), first, second)

    return read


def product_at(refs, names, place, pair, rows):
    first, second = pair
    if first == -second != 0:
        return refs[names.index((second, 0))][rows, :] * refs[names.index((second, 1))][rows, :]
    read = orbital_at(refs, names, place, rows)
    value = read(first)
    return value * (value if first == second else read(second))


def views(refs, place):
    if len(refs) > 1:
        return refs
    return [refs[0].at[place[1] ^ step] for step in STEPS]


def spread_kernel(pairs, names, place, *refs):
    orbitals, (lines, columns), outs = refs[: len(names)], refs[len(names) : len(names) + 2], refs[len(names) + 2 : -1]
    outs, work = views(outs, place), refs[-1]
    lane = lane_index(GROUPS)
    for index, pair in enumerate(pairs):

        def load(tile, pair=pair):
            return product_at(orbitals, names, place, pair, pl.ds(tile, GROUPS, stride=9))

        def store(line, value, index=index):
            work[pl.ds(index * LINES + line, GROUPS, stride=16), :] = value

        unpack(16, load, store, lane)
    line_passes(work, lines, len(pairs))
    column_passes(work, columns, len(pairs))
    lane = lane_index(PLANES)
    for index in range(len(pairs)):
        for out, step in zip(outs, STEPS):
            first = (place[1] ^ step) * PLANES + index * LINES

            def load(line, first=first):
                return work[pl.ds(first + line, PLANES, stride=G), :]

            def store(tile, value, start=index * PAIR_ROWS, out=out):
                out[start + tile * PLANES : start + (tile + 1) * PLANES, :] = value

            pack(PLANES, load, store, lane)
            start = index * PAIR_ROWS + TILES * PLANES
            out[start : start + 2, :] = jnp.zeros((2, LANES), jnp.float32)


def pencil_kernel(count, parts, place, *refs):
    chunks, (kernel, forward, backward), outs = refs[:parts], refs[parts : parts + 3], refs[parts + 3 :]
    chunks = views(chunks, place)
    forward, backward = forward.at[place[1]], backward.at[place[1]]
    lane = lane_index(G)
    gap = jnp.zeros((STEP - PLANES, LANES), jnp.float32)
    energies = [jnp.zeros((G, LANES), jnp.float32) for _ in range(count)]
    places = [(pair, tile) for tile in range(TILES) for pair in range(count)]
    for group in range(0, len(places), 2):
        now = places[group : group + 2]
        values = []
        for pair, tile in now:
            start = pair * PAIR_ROWS + tile * PLANES
            pieces = []
            for chunk in chunks:
                pieces += [chunk[start : start + PLANES, :], gap]
            values.append(jnp.concatenate(pieces, axis=0))
        solved = []
        for (pair, tile), spectral in zip(now, along_columns(values, forward[...])):
            solved.append(spectral * kernel[:, tile * LANES : (tile + 1) * LANES])
            if tile == TILES - 1:
                spectral = jnp.where(lane < PLANES * G - tile * LANES, spectral, 0.0)
            energies[pair] = energies[pair] + spectral * solved[-1]
        for (pair, tile), value in zip(now, along_columns(solved, backward[...])):
            start = pair * PAIR_ROWS + tile * PLANES
            for index, out in enumerate(outs):
                out[start : start + PLANES, :] = value[index * STEP : index * STEP + PLANES]
    for pair in range(count):
        total = jnp.full((2, LANES), jnp.sum(energies[pair]), jnp.float32)
        start = pair * PAIR_ROWS + TILES * PLANES
        for out in outs:
            out[start : start + 2, :] = total


def gather_kernel(count, parts, names, shares, place, *refs):
    chunks, (lines, columns), refs = views(refs[:parts], place), refs[parts : parts + 2], refs[parts + 2 :]
    orbitals = refs[: len(names)]
    outs, work = refs[-1 - len(shares) : -1], refs[-1]
    outs = dict(zip(shares, outs))
    added = dict(zip((2, -2), refs[len(names) : -1 - len(shares)]))
    upward = place[0] == 0
    lane = lane_index(PLANES)
    for pair in range(count):
        for chunk, step in zip(chunks, STEPS):
            first = pair * LINES + (place[1] ^ step) * PLANES

            def load(tile, start=pair * PAIR_ROWS, chunk=chunk):
                return chunk[start + tile * PLANES : start + (tile + 1) * PLANES, :]

            def store(line, value, first=first):
                work[pl.ds(first + line, PLANES, stride=G), :] = value

            unpack(PLANES, load, store, lane)
    column_passes(work, columns, count)
    line_passes(work, lines, count)
    lane = lane_index(GROUPS)

    def write(rows, terms, begun):
        shape = next(iter(terms.values())).shape
        for name in (1, 2):
            if name in terms or -name in terms:
                ahead = terms.get(name, jnp.zeros(shape, jnp.float32))
                behind = terms.get(-name, jnp.zeros(shape, jnp.float32))
                terms[name] = jnp.where(upward, ahead, behind)
                terms[-name] = jnp.where(upward, behind, ahead)
        for name, term in terms.items():
            if name in begun:
                term = term + outs[name][rows, :]
            elif name in added:
                term = term + added[name][rows, :]
            outs[name][rows, :] = term
        return set(terms)

    begun = set()
    for pair in range(count):

        def load(line, start=pair * LINES):
            return work[pl.ds(start + line, GROUPS, stride=16), :]

        written = set()

        def store(tile, value, pair=pair, written=written):
            rows = pl.ds(tile, GROUPS, stride=9)
            read = orbital_at(orbitals, names, place, rows)
            terms = {}
            for name, share in shares.items():
                for other, distance in share:
                    if other == pair:
                        terms[name] = value * read(distance)
            written |= write(rows, terms, begun)

        pack(16, load, store, lane)
        begun |= written
    totals = {}
    for name, share in shares.items():
        total = jnp.zeros((1, LANES), jnp.float32)
        for pair, _ in share:
            start = pair * PAIR_ROWS + TILES * PLANES
            for device in range(DEVICES):
                total = total + device_row(chunks, place, device, start)
        totals[name] = jnp.broadcast_to(total, (PAD_ROWS - ROWS, LANES))
    write(slice(ROWS, PAD_ROWS), totals, set())


def enter_kernel(cells, out):
    whole = ROWS // 8 * 8
    for row in range(0, whole, 8):
        out[row : row + 8, :] = cells[:, row * LANES : (row + 8) * LANES].reshape(8, LANES)
    out[whole:ROWS, :] = cells[:, whole * LANES :]
    out[ROWS:, :] = jnp.ones((PAD_ROWS - ROWS, LANES), jnp.float32)


def leave_kernel(own, *refs):
    parts, (residual, intersection) = refs[:-2], refs[-2:]

    def exchange(rows):
        return -FRACTION * sum(part[rows, :] for part in parts)

    mean = exchange(slice(ROWS, ROWS + 1)) * (1.0 / CELLS)
    intersection[...] = mean[:, :1]
    whole = ROWS // 8 * 8
    for row in range(0, whole, 8):
        rows = slice(row, row + 8)
        value = exchange(rows) - mean * own[rows, :]
        residual[:, row * LANES : (row + 8) * LANES] = value.reshape(1, 8 * LANES)
    rows = slice(whole, ROWS)
    residual[:, whole * LANES :] = exchange(rows) - mean * own[rows, :]


VMEM = pl.BlockSpec(memory_space=pltpu.VMEM)
SMEM = pl.BlockSpec(memory_space=pltpu.SMEM)
PARAMS = pltpu.CompilerParams(vmem_limit_bytes=8 * 1024 * 1024)


def chunks_of(count, parts):
    rows = count * PAIR_ROWS
    if parts == 1:
        return [jax.ShapeDtypeStruct((DEVICES, rows, LANES), jnp.float32)]
    return [jax.ShapeDtypeStruct((rows, LANES), jnp.float32)] * parts


def work_of(count):
    return [pltpu.VMEM((count * LINES, LANES), jnp.float32)]


def spread_pairs(orbitals, pairs, tables, parts=DEVICES):
    return pl.pallas_call(
        lambda *refs: spread_kernel(pairs, list(orbitals), *refs),
        out_shape=chunks_of(len(pairs), parts),
        in_specs=[SMEM] + [VMEM] * (len(orbitals) + 2),
        out_specs=[VMEM] * parts,
        scratch_shapes=work_of(len(pairs)),
        compiler_params=PARAMS,
        name="spread",
    )(tables["place"], *orbitals.values(), tables["lines"], tables["columns"])


def solve_pencils(chunks, count, tables):
    parts = len(chunks)
    return pl.pallas_call(
        lambda *refs: pencil_kernel(count, parts, *refs),
        out_shape=chunks_of(count, DEVICES),
        in_specs=[SMEM] + [VMEM] * (parts + 3),
        out_specs=[VMEM] * DEVICES,
        compiler_params=PARAMS,
        name="pencils",
    )(tables["place"], *chunks, tables["kernel"], tables["forward"], tables["backward"])


def gather_shares(chunks, count, orbitals, shares, tables, added=()):
    parts = len(chunks)
    return pl.pallas_call(
        lambda *refs: gather_kernel(count, parts, list(orbitals), shares, *refs),
        out_shape=[jax.ShapeDtypeStruct((PAD_ROWS, LANES), jnp.float32)] * len(shares),
        in_specs=[SMEM] + [VMEM] * (parts + 2 + len(orbitals) + len(added)),
        out_specs=[VMEM] * len(shares),
        scratch_shapes=work_of(count),
        compiler_params=PARAMS,
        name="gather",
    )(tables["place"], *chunks, tables["lines"], tables["columns"], *orbitals.values(), *added)


def enter(cells):
    return pl.pallas_call(
        enter_kernel,
        out_shape=jax.ShapeDtypeStruct((PAD_ROWS, LANES), jnp.float32),
        in_specs=[VMEM],
        out_specs=VMEM,
        compiler_params=PARAMS,
        name="enter",
    )(cells)


def leave(own, *parts):
    return pl.pallas_call(
        leave_kernel,
        out_shape=[jax.ShapeDtypeStruct((1, ROWS * LANES), jnp.float32), jax.ShapeDtypeStruct((1, 1), jnp.float32)],
        in_specs=[VMEM] * (1 + len(parts)),
        out_specs=[VMEM] * 2,
        compiler_params=PARAMS,
        name="leave",
    )(own, *parts)


def exchanged(chunks):
    if len(chunks) == 1:
        return [lax.all_to_all(chunks[0], "grid", split_axis=0, concat_axis=0)]
    received = [chunks[0]]
    for chunk, step in zip(chunks[1:], STEPS[1:]):
        pairs = [(device, device ^ step) for device in range(DEVICES)]
        received.append(lax.ppermute(chunk, "grid", pairs))
    return received


def after(values, *others):
    return lax.optimization_barrier((values, others))[0]


def swapped(value, step, phase):
    count = lax.axis_size("orb")
    pairs = []
    for source in range(count):
        upward = source // step % 2 == phase
        pairs.append((source, (source + (step if upward else -step)) % count))
    return lax.ppermute(value, "orb", pairs)


def shards(orbitals):
    device = lax.axis_index("grid")
    block = lax.axis_index("orb")
    tables = {
        "place": jnp.stack([block % 2, device]).astype(jnp.int32),
        "kernel": screened(device),
        "lines": jnp.asarray(line_weights()),
        "columns": jnp.asarray(column_weights()),
        "forward": jnp.asarray(np.stack([forward_weights(d) for d in range(DEVICES)])),
        "backward": jnp.asarray(np.stack([backward_weights(d) for d in range(DEVICES)])),
    }
    own = enter(orbitals)
    second = swapped(own, 1, 1)
    first = swapped(own, 1, 0)
    third = swapped(first, 1, 1)
    fourth = swapped(second, 1, 0)
    close = {0: own, (1, 0): first, (1, 1): second}
    near = spread_pairs(close, [(0, 1), (-1, 1)], tables)
    third, fourth = after((third, fourth), near)
    wide = {(1, 0): first, (1, 1): second, (2, 0): third, (2, 1): fourth}
    far = spread_pairs(wide, [(-1, 2), (-2, 2)], tables)
    none = spread_pairs({0: after(own, far)}, [(0, 0)], tables)
    near = solve_pencils(exchanged(near), 2, tables)
    far = solve_pencils(after(exchanged(far), near, none), 2, tables)
    near = exchanged(near)
    far = exchanged(far)
    shares = {1: [(0, 0), (1, -1)], -1: [(1, 1)], 0: [(0, 1)]}
    three, four, kept = gather_shares(near, 2, close, shares, tables)
    none = exchanged(after(none, kept))
    far = after(far, kept)
    shares = {1: [(0, -1), (1, -2)], -1: [(1, 2)], 2: [], -2: [(0, 2)]}
    one, two, three, four = gather_shares(far, 2, wide, shares, tables, [three, four])
    one = swapped(after(one, none), 1, 0)
    two = swapped(two, 1, 1)
    none = solve_pencils(none, 1, tables)
    four = swapped(one + four, 1, 1)
    three = swapped(two + after(three, none), 1, 0)
    none = exchanged(none)
    kept = kept + four
    (self_share,) = gather_shares(none, 1, {0: own}, {0: [(0, 0)]}, tables)
    residual, intersection = leave(own, self_share, kept, three)
    return residual, intersection.reshape(1, 1, 1)


def solution(mesh):
    in_specs = (P("orb", "grid"),)
    out_specs = (P("orb", "grid"), P("orb", None, None))
    return jax.shard_map(shards, mesh=mesh, in_specs=in_specs, out_specs=out_specs, check_vma=False)
```

```python
import math

import jax
import jax.numpy as jnp
import numpy as np
from jax import lax
from jax.experimental import pallas as pl
from jax.experimental.pallas import tpu as pltpu
from jax.sharding import PartitionSpec as P

G = 72
LANES = 128
DEVICES = 4
STEPS = (0, 2, 3, 1)
PLANES = G // DEVICES
LINES = PLANES * G
ROWS = LINES * G // LANES
PAD_ROWS = 736
GROUPS = ROWS // 9
TILES = 11
PAIR_ROWS = 200
STEP = 24
SCREENING = 0.09
FRACTION = 0.25
CELLS = float(G * G * G)


def hartley_halves():
    indices = np.arange(G)
    phases = 2.0 * np.pi * (indices[:, None] * indices[None, :] % G) / G
    table = np.cos(phases) + np.sin(phases)
    high = table.astype(jnp.bfloat16)
    low = (table - high.astype(np.float64)).astype(jnp.bfloat16)
    return high, low


def line_weights():
    high, low = hartley_halves()
    weights = np.zeros((2 * LANES, 2 * LANES), jnp.bfloat16)
    weights[:G, :G] = high
    weights[:G, LANES : LANES + G] = low
    weights[LANES : LANES + G, :G] = high
    return weights


def column_weights():
    return np.concatenate(hartley_halves(), axis=0)


def spread(table):
    wide = np.zeros((G, DEVICES * STEP), jnp.bfloat16)
    for device in range(DEVICES):
        wide[:, device * STEP : device * STEP + PLANES] = table[:, device * PLANES : (device + 1) * PLANES]
    return wide


def in_order(table, device):
    blocks = np.split(table, DEVICES, axis=1)
    return np.concatenate([blocks[device ^ step] for step in STEPS], axis=1)


def forward_weights(device):
    return np.concatenate([spread(in_order(half, device)) for half in hartley_halves()], axis=0)


def backward_weights(device):
    return np.concatenate([spread(in_order(half, device)).T for half in hartley_halves()], axis=0)


def wavenumber(indices):
    return jnp.minimum(indices, G - indices).astype(jnp.float32) * (2.0 * math.pi / G)


def screened(device):
    lanes = jnp.arange(TILES * LANES, dtype=jnp.int32)
    first = wavenumber(jnp.arange(G, dtype=jnp.int32))
    second = wavenumber(jnp.minimum(device * PLANES + lanes // G, G - 1))
    third = wavenumber(lanes % G)
    squared = first[:, None] ** 2 + (second**2)[None, :] + (third**2)[None, :]
    scaled = squared / (4.0 * SCREENING * SCREENING)
    guarded = jnp.where(scaled > 0, scaled, 1.0)
    return jnp.where(scaled > 0, (1.0 - jnp.exp(-guarded)) / guarded, 1.0) / CELLS


def halves(value):
    high = value.astype(jnp.bfloat16)
    return high, (value - high.astype(jnp.float32)).astype(jnp.bfloat16)


def product(left, right):
    return jnp.dot(left, right, preferred_element_type=jnp.float32)


def along_lines(value, weights):
    result = product(jnp.concatenate(halves(value), axis=1), weights)
    return result[:, :LANES] + result[:, LANES:]


def along_columns(values, weights):
    rows = weights.shape[0] // 2
    high, low = halves(jnp.concatenate(values, axis=1) if len(values) > 1 else values[0])
    result = product(weights, high)
    result = result[:rows] + result[rows:] + product(weights[:rows], low)
    return [result[:, index * LANES : (index + 1) * LANES] for index in range(len(values))]


def unpack(lines, load, store, lane):
    tiles = {}

    def tile_at(tile):
        if tile not in tiles:
            tiles.pop(tile - 2, None)
            tiles[tile] = load(tile)
        return tiles[tile]

    for line in range(lines):
        tile, shift = divmod(line * G, LANES)
        value = tile_at(tile)
        if shift:
            value = pltpu.roll(value, LANES - shift, 1)
        if shift + G > LANES:
            tail = pltpu.roll(tile_at(tile + 1), LANES - shift, 1)
            value = jnp.where(lane < LANES - shift, value, tail)
        store(line, jnp.where(lane < G, value, 0.0))


def pack(lines, load, store, lane):
    filled = jnp.zeros(lane.shape, jnp.float32)
    for line in range(lines):
        tile, shift = divmod(line * G, LANES)
        value = load(line)
        if shift:
            value = pltpu.roll(value, shift, 1)
        if shift + G < LANES:
            filled = filled + value
            if line == lines - 1:
                store(tile, filled)
            continue
        store(tile, filled + jnp.where(lane >= shift, value, 0.0))
        filled = jnp.where(lane < shift, value, 0.0)
        if line == lines - 1 and shift + G > LANES:
            store(tile + 1, filled)


def lane_index(rows):
    return lax.broadcasted_iota(jnp.int32, (rows, LANES), 1)


def line_passes(work, weights, count):
    rows = 6 * G

    def some_lines(index, carry):
        block = pl.ds(pl.multiple_of(index * rows, 8), rows)
        work[block, :] = along_lines(work[block, :], weights[...])
        return carry

    lax.fori_loop(0, count * LINES // rows, some_lines, 0, unroll=True)


def column_passes(source, target, count, weights):
    def planes(index, carry):
        blocks = [2 * index + half for half in range(2)]
        values = along_columns([source[0][source[1](plane), :] for plane in blocks], weights[...])
        for plane, value in zip(blocks, values):
            target[0][target[1](plane), :] = value
        return carry

    lax.fori_loop(0, count * PLANES // 2, planes, 0, unroll=3)


def whole_plane(plane):
    return pl.ds(pl.multiple_of(plane * G, 8), G)


def spread_plane(count):
    return lambda plane: pl.ds(plane, G, stride=count * PLANES + 1)


def device_row(chunks, place, device, row):
    value = chunks[0][row : row + 1, :]
    for chunk, step in zip(chunks[1:], STEPS[1:]):
        value = jnp.where(place[1] ^ step == device, chunk[row : row + 1, :], value)
    return value


def orbital_at(refs, names, place, rows):
    def read(distance):
        if distance in names:
            return refs[names.index(distance)][rows, :]
        step = abs(distance)
        first = refs[names.index((step, 0))][rows, :]
        second = refs[names.index((step, 1))][rows, :]
        upward = place[0] == (0 if step == 1 else 1)
        return jnp.where(upward if distance > 0 else jnp.logical_not(upward), first, second)

    return read


def product_at(refs, names, place, pair, rows):
    first, second = pair
    if first == -second != 0:
        return refs[names.index((second, 0))][rows, :] * refs[names.index((second, 1))][rows, :]
    read = orbital_at(refs, names, place, rows)
    value = read(first)
    return value * (value if first == second else read(second))


def views(refs, place):
    if len(refs) > 1:
        return refs
    return [refs[0].at[place[1] ^ step] for step in STEPS]


def spread_kernel(pairs, names, place, *refs):
    orbitals, (lines, columns), outs = refs[: len(names)], refs[len(names) : len(names) + 2], refs[len(names) + 2 : -1]
    outs, work, turned = views(outs[:-1], place), refs[-2], refs[-1]
    wide = len(pairs) * PLANES + 1
    lane = lane_index(GROUPS)
    for index, pair in enumerate(pairs):

        def load(tile, pair=pair):
            return product_at(orbitals, names, place, pair, pl.ds(tile, GROUPS, stride=9))

        def store(line, value, index=index):
            work[pl.ds(index * LINES + line, GROUPS, stride=16), :] = value

        unpack(16, load, store, lane)
    line_passes(work, lines, len(pairs))
    column_passes((work, whole_plane), (turned, spread_plane(len(pairs))), len(pairs), columns)
    lane = lane_index(PLANES)
    for index in range(len(pairs)):
        for out, step in zip(outs, STEPS):
            first = (place[1] ^ step) * PLANES * wide + index * PLANES

            def load(line, first=first):
                return turned[pl.ds(first + line * wide, PLANES), :]

            def store(tile, value, start=index * PAIR_ROWS, out=out):
                out[start + tile * PLANES : start + (tile + 1) * PLANES, :] = value

            pack(PLANES, load, store, lane)
            start = index * PAIR_ROWS + TILES * PLANES
            out[start : start + 2, :] = jnp.zeros((2, LANES), jnp.float32)


def pencil_kernel(count, parts, place, *refs):
    chunks, (kernel, forward, backward), outs = refs[:parts], refs[parts : parts + 3], refs[parts + 3 :]
    chunks = views(chunks, place)
    forward, backward = forward.at[place[1]], backward.at[place[1]]
    lane = lane_index(G)
    gap = jnp.zeros((STEP - PLANES, LANES), jnp.float32)
    energies = [jnp.zeros((G, LANES), jnp.float32) for _ in range(count)]
    places = [(pair, tile) for tile in range(TILES) for pair in range(count)]
    for group in range(0, len(places), 2):
        now = places[group : group + 2]
        values = []
        for pair, tile in now:
            start = pair * PAIR_ROWS + tile * PLANES
            pieces = []
            for chunk in chunks:
                pieces += [chunk[start : start + PLANES, :], gap]
            values.append(jnp.concatenate(pieces, axis=0))
        solved = []
        for (pair, tile), spectral in zip(now, along_columns(values, forward[...])):
            solved.append(spectral * kernel[:, tile * LANES : (tile + 1) * LANES])
            if tile == TILES - 1:
                spectral = jnp.where(lane < PLANES * G - tile * LANES, spectral, 0.0)
            energies[pair] = energies[pair] + spectral * solved[-1]
        for (pair, tile), value in zip(now, along_columns(solved, backward[...])):
            start = pair * PAIR_ROWS + tile * PLANES
            for index, out in enumerate(outs):
                out[start : start + PLANES, :] = value[index * STEP : index * STEP + PLANES]
    for pair in range(count):
        total = jnp.full((2, LANES), jnp.sum(energies[pair]), jnp.float32)
        start = pair * PAIR_ROWS + TILES * PLANES
        for out in outs:
            out[start : start + 2, :] = total


def gather_kernel(count, parts, names, shares, place, *refs):
    chunks, (lines, columns), refs = views(refs[:parts], place), refs[parts : parts + 2], refs[parts + 2 :]
    orbitals = refs[: len(names)]
    outs, work, turned = refs[-2 - len(shares) : -2], refs[-2], refs[-1]
    outs = dict(zip(shares, outs))
    added = dict(zip((2, -2), refs[len(names) : -2 - len(shares)]))
    wide = count * PLANES + 1
    upward = place[0] == 0
    lane = lane_index(PLANES)
    for pair in range(count):
        for chunk, step in zip(chunks, STEPS):
            first = (place[1] ^ step) * PLANES * wide + pair * PLANES

            def load(tile, start=pair * PAIR_ROWS, chunk=chunk):
                return chunk[start + tile * PLANES : start + (tile + 1) * PLANES, :]

            def store(line, value, first=first):
                turned[pl.ds(first + line * wide, PLANES), :] = value

            unpack(PLANES, load, store, lane)
    column_passes((turned, spread_plane(count)), (work, whole_plane), count, columns)
    line_passes(work, lines, count)
    lane = lane_index(GROUPS)

    def write(rows, terms, begun):
        shape = next(iter(terms.values())).shape
        for name in (1, 2):
            if name in terms or -name in terms:
                ahead = terms.get(name, jnp.zeros(shape, jnp.float32))
                behind = terms.get(-name, jnp.zeros(shape, jnp.float32))
                terms[name] = jnp.where(upward, ahead, behind)
                terms[-name] = jnp.where(upward, behind, ahead)
        for name, term in terms.items():
            if name in begun:
                term = term + outs[name][rows, :]
            elif name in added:
                term = term + added[name][rows, :]
            outs[name][rows, :] = term
        return set(terms)

    begun = set()
    for pair in range(count):

        def load(line, start=pair * LINES):
            return work[pl.ds(start + line, GROUPS, stride=16), :]

        written = set()

        def store(tile, value, pair=pair, written=written):
            rows = pl.ds(tile, GROUPS, stride=9)
            read = orbital_at(orbitals, names, place, rows)
            terms = {}
            for name, share in shares.items():
                for other, distance in share:
                    if other == pair:
                        terms[name] = value * read(distance)
            written |= write(rows, terms, begun)

        pack(16, load, store, lane)
        begun |= written
    totals = {}
    for name, share in shares.items():
        total = jnp.zeros((1, LANES), jnp.float32)
        for pair, _ in share:
            start = pair * PAIR_ROWS + TILES * PLANES
            for device in range(DEVICES):
                total = total + device_row(chunks, place, device, start)
        totals[name] = jnp.broadcast_to(total, (PAD_ROWS - ROWS, LANES))
    write(slice(ROWS, PAD_ROWS), totals, set())


def enter_kernel(cells, out):
    whole = ROWS // 8 * 8
    for row in range(0, whole, 8):
        out[row : row + 8, :] = cells[:, row * LANES : (row + 8) * LANES].reshape(8, LANES)
    out[whole:ROWS, :] = cells[:, whole * LANES :]
    out[ROWS:, :] = jnp.ones((PAD_ROWS - ROWS, LANES), jnp.float32)


def leave_kernel(own, *refs):
    parts, (residual, intersection) = refs[:-2], refs[-2:]

    def exchange(rows):
        return -FRACTION * sum(part[rows, :] for part in parts)

    mean = exchange(slice(ROWS, ROWS + 1)) * (1.0 / CELLS)
    intersection[...] = mean[:, :1]
    whole = ROWS // 8 * 8
    for row in range(0, whole, 8):
        rows = slice(row, row + 8)
        value = exchange(rows) - mean * own[rows, :]
        residual[:, row * LANES : (row + 8) * LANES] = value.reshape(1, 8 * LANES)
    rows = slice(whole, ROWS)
    residual[:, whole * LANES :] = exchange(rows) - mean * own[rows, :]


VMEM = pl.BlockSpec(memory_space=pltpu.VMEM)
SMEM = pl.BlockSpec(memory_space=pltpu.SMEM)
PARAMS = pltpu.CompilerParams(vmem_limit_bytes=8 * 1024 * 1024)


def chunks_of(count, parts):
    rows = count * PAIR_ROWS
    if parts == 1:
        return [jax.ShapeDtypeStruct((DEVICES, rows, LANES), jnp.float32)]
    return [jax.ShapeDtypeStruct((rows, LANES), jnp.float32)] * parts


def work_of(count):
    turned = G * (count * PLANES + 1) + 7
    return [pltpu.VMEM((rows, LANES), jnp.float32) for rows in (count * LINES, turned)]


def spread_pairs(orbitals, pairs, tables, parts=DEVICES):
    return pl.pallas_call(
        lambda *refs: spread_kernel(pairs, list(orbitals), *refs),
        out_shape=chunks_of(len(pairs), parts),
        in_specs=[SMEM] + [VMEM] * (len(orbitals) + 2),
        out_specs=[VMEM] * parts,
        scratch_shapes=work_of(len(pairs)),
        compiler_params=PARAMS,
        name="spread",
    )(tables["place"], *orbitals.values(), tables["lines"], tables["columns"])


def solve_pencils(chunks, count, tables):
    parts = len(chunks)
    return pl.pallas_call(
        lambda *refs: pencil_kernel(count, parts, *refs),
        out_shape=chunks_of(count, DEVICES),
        in_specs=[SMEM] + [VMEM] * (parts + 3),
        out_specs=[VMEM] * DEVICES,
        compiler_params=PARAMS,
        name="pencils",
    )(tables["place"], *chunks, tables["kernel"], tables["forward"], tables["backward"])


def gather_shares(chunks, count, orbitals, shares, tables, added=()):
    parts = len(chunks)
    return pl.pallas_call(
        lambda *refs: gather_kernel(count, parts, list(orbitals), shares, *refs),
        out_shape=[jax.ShapeDtypeStruct((PAD_ROWS, LANES), jnp.float32)] * len(shares),
        in_specs=[SMEM] + [VMEM] * (parts + 2 + len(orbitals) + len(added)),
        out_specs=[VMEM] * len(shares),
        scratch_shapes=work_of(count),
        compiler_params=PARAMS,
        name="gather",
    )(tables["place"], *chunks, tables["lines"], tables["columns"], *orbitals.values(), *added)


def enter(cells):
    return pl.pallas_call(
        enter_kernel,
        out_shape=jax.ShapeDtypeStruct((PAD_ROWS, LANES), jnp.float32),
        in_specs=[VMEM],
        out_specs=VMEM,
        compiler_params=PARAMS,
        name="enter",
    )(cells)


def leave(own, *parts):
    return pl.pallas_call(
        leave_kernel,
        out_shape=[jax.ShapeDtypeStruct((1, ROWS * LANES), jnp.float32), jax.ShapeDtypeStruct((1, 1), jnp.float32)],
        in_specs=[VMEM] * (1 + len(parts)),
        out_specs=[VMEM] * 2,
        compiler_params=PARAMS,
        name="leave",
    )(own, *parts)


def exchanged(chunks):
    if len(chunks) == 1:
        return [lax.all_to_all(chunks[0], "grid", split_axis=0, concat_axis=0)]
    received = [chunks[0]]
    for chunk, step in zip(chunks[1:], STEPS[1:]):
        pairs = [(device, device ^ step) for device in range(DEVICES)]
        received.append(lax.ppermute(chunk, "grid", pairs))
    return received


def after(values, *others):
    return lax.optimization_barrier((values, others))[0]


def swapped(value, step, phase):
    count = lax.axis_size("orb")
    pairs = []
    for source in range(count):
        upward = source // step % 2 == phase
        pairs.append((source, (source + (step if upward else -step)) % count))
    return lax.ppermute(value, "orb", pairs)


def shards(orbitals):
    device = lax.axis_index("grid")
    block = lax.axis_index("orb")
    tables = {
        "place": jnp.stack([block % 2, device]).astype(jnp.int32),
        "kernel": screened(device),
        "lines": jnp.asarray(line_weights()),
        "columns": jnp.asarray(column_weights()),
        "forward": jnp.asarray(np.stack([forward_weights(d) for d in range(DEVICES)])),
        "backward": jnp.asarray(np.stack([backward_weights(d) for d in range(DEVICES)])),
    }
    own = enter(orbitals)
    second = swapped(own, 1, 1)
    first = swapped(own, 1, 0)
    third = swapped(first, 1, 1)
    fourth = swapped(second, 1, 0)
    close = {0: own, (1, 0): first, (1, 1): second}
    near = spread_pairs(close, [(0, 1), (-1, 1)], tables)
    third, fourth = after((third, fourth), near)
    wide = {(1, 0): first, (1, 1): second, (2, 0): third, (2, 1): fourth}
    far = spread_pairs(wide, [(-1, 2), (-2, 2)], tables)
    none = spread_pairs({0: after(own, far)}, [(0, 0)], tables)
    near = solve_pencils(exchanged(near), 2, tables)
    far = solve_pencils(after(exchanged(far), near, none), 2, tables)
    near = exchanged(near)
    far = exchanged(far)
    shares = {1: [(0, 0), (1, -1)], -1: [(1, 1)], 0: [(0, 1)]}
    three, four, kept = gather_shares(near, 2, close, shares, tables)
    none = exchanged(after(none, kept))
    far = after(far, kept)
    shares = {1: [(0, -1), (1, -2)], -1: [(1, 2)], 2: [], -2: [(0, 2)]}
    one, two, three, four = gather_shares(far, 2, wide, shares, tables, [three, four])
    one = swapped(after(one, none), 1, 0)
    two = swapped(two, 1, 1)
    none = solve_pencils(none, 1, tables)
    four = swapped(one + four, 1, 1)
    three = swapped(two + after(three, none), 1, 0)
    none = exchanged(none)
    kept = kept + four
    (self_share,) = gather_shares(none, 1, {0: own}, {0: [(0, 0)]}, tables)
    residual, intersection = leave(own, self_share, kept, three)
    return residual, intersection.reshape(1, 1, 1)


def solution(mesh):
    in_specs = (P("orb", "grid"),)
    out_specs = (P("orb", "grid"), P("orb", None, None))
    return jax.shard_map(shards, mesh=mesh, in_specs=in_specs, out_specs=out_specs, check_vma=False)
```

```python
import math

import jax
import jax.numpy as jnp
import numpy as np
from jax import lax
from jax.experimental import pallas as pl
from jax.experimental.pallas import tpu as pltpu
from jax.sharding import PartitionSpec as P

G = 72
LANES = 128
DEVICES = 4
STEPS = (0, 2, 3, 1)
PLANES = G // DEVICES
LINES = PLANES * G
ROWS = LINES * G // LANES
PAD_ROWS = 736
GROUPS = ROWS // 9
TILES = 11
PAIR_ROWS = 200
STEP = 24
DEPTH = 80
SCREENING = 0.09
FRACTION = 0.25
CELLS = float(G * G * G)


def hartley_halves():
    indices = np.arange(G)
    phases = 2.0 * np.pi * (indices[:, None] * indices[None, :] % G) / G
    table = np.cos(phases) + np.sin(phases)
    high = table.astype(jnp.bfloat16)
    low = (table - high.astype(np.float64)).astype(jnp.bfloat16)
    return high, low


def line_weights():
    high, low = hartley_halves()
    weights = np.zeros((2 * LANES, 2 * LANES), jnp.bfloat16)
    weights[:G, :G] = high
    weights[:G, LANES : LANES + G] = low
    weights[LANES : LANES + G, :G] = high
    return weights


def stacked(left):
    gap = np.zeros((left[0].shape[0], DEPTH - G), jnp.bfloat16)
    high, low = left
    return np.concatenate([high, gap, low, gap, high, gap], axis=1)


def padded(table, rows):
    return np.concatenate([table, np.zeros((rows - table.shape[0], table.shape[1]), table.dtype)], axis=0)


def column_weights():
    return padded(stacked(hartley_halves()), DEPTH)


def in_order(table, device):
    blocks = np.split(table, DEVICES, axis=1)
    return [blocks[device ^ step] for step in STEPS]


def forward_weights(device):
    halves_in_order = [np.concatenate(in_order(half, device), axis=1) for half in hartley_halves()]
    return padded(stacked(halves_in_order), DEPTH)


def backward_weights(device):
    spread = []
    for half in hartley_halves():
        spread.append(np.concatenate([padded(block.T, STEP) for block in in_order(half, device)], axis=0))
    return stacked(spread)


def wavenumber(indices):
    return jnp.minimum(indices, G - indices).astype(jnp.float32) * (2.0 * math.pi / G)


def screened(device):
    lanes = jnp.arange(TILES * LANES, dtype=jnp.int32)
    first = wavenumber(jnp.arange(G, dtype=jnp.int32))
    second = wavenumber(jnp.minimum(device * PLANES + lanes // G, G - 1))
    third = wavenumber(lanes % G)
    squared = first[:, None] ** 2 + (second**2)[None, :] + (third**2)[None, :]
    scaled = squared / (4.0 * SCREENING * SCREENING)
    guarded = jnp.where(scaled > 0, scaled, 1.0)
    return jnp.where(scaled > 0, (1.0 - jnp.exp(-guarded)) / guarded, 1.0) / CELLS


def halves(value):
    high = value.astype(jnp.bfloat16)
    return high, (value - high.astype(jnp.float32)).astype(jnp.bfloat16)


def product(left, right):
    return jnp.dot(left, right, preferred_element_type=jnp.float32)


def along_lines(value, weights):
    result = product(jnp.concatenate(halves(value), axis=1), weights)
    return result[:, :LANES] + result[:, LANES:]


def along_columns(values, weights):
    value = jnp.concatenate(values, axis=1) if len(values) > 1 else values[0]
    value = jnp.concatenate([value, jnp.zeros((DEPTH - G, value.shape[1]), jnp.float32)], axis=0)
    high, low = halves(value)
    result = product(weights, jnp.concatenate([high, high, low], axis=0))
    return [result[:, index * LANES : (index + 1) * LANES] for index in range(len(values))]


def unpack(lines, load, store, lane):
    tiles = {}

    def tile_at(tile):
        if tile not in tiles:
            tiles.pop(tile - 2, None)
            tiles[tile] = load(tile)
        return tiles[tile]

    for line in range(lines):
        tile, shift = divmod(line * G, LANES)
        value = tile_at(tile)
        if shift:
            value = pltpu.roll(value, LANES - shift, 1)
        if shift + G > LANES:
            tail = pltpu.roll(tile_at(tile + 1), LANES - shift, 1)
            value = jnp.where(lane < LANES - shift, value, tail)
        store(line, jnp.where(lane < G, value, 0.0))


def pack(lines, load, store, lane):
    filled = jnp.zeros(lane.shape, jnp.float32)
    for line in range(lines):
        tile, shift = divmod(line * G, LANES)
        value = load(line)
        if shift:
            value = pltpu.roll(value, shift, 1)
        if shift + G < LANES:
            filled = filled + value
            if line == lines - 1:
                store(tile, filled)
            continue
        store(tile, filled + jnp.where(lane >= shift, value, 0.0))
        filled = jnp.where(lane < shift, value, 0.0)
        if line == lines - 1 and shift + G > LANES:
            store(tile + 1, filled)


def lane_index(rows):
    return lax.broadcasted_iota(jnp.int32, (rows, LANES), 1)


def line_passes(work, weights, count):
    rows = 6 * G

    def some_lines(index, carry):
        block = pl.ds(pl.multiple_of(index * rows, 8), rows)
        work[block, :] = along_lines(work[block, :], weights[...])
        return carry

    lax.fori_loop(0, count * LINES // rows, some_lines, 0, unroll=True)


def column_passes(work, weights, count):
    def planes(index, carry):
        blocks = [pl.ds(pl.multiple_of((2 * index + half) * G, 8), G) for half in range(2)]
        values = along_columns([work[block, :] for block in blocks], weights[...])
        for block, value in zip(blocks, values):
            work[block, :] = value[:G]
        return carry

    lax.fori_loop(0, count * PLANES // 2, planes, 0, unroll=3)


def device_row(chunks, place, device, row):
    value = chunks[0][row : row + 1, :]
    for chunk, step in zip(chunks[1:], STEPS[1:]):
        value = jnp.where(place[1] ^ step == device, chunk[row : row + 1, :], value)
    return value


def orbital_at(refs, names, place, rows):
    def read(distance):
        if distance in names:
            return refs[names.index(distance)][rows, :]
        step = abs(distance)
        first = refs[names.index((step, 0))][rows, :]
        second = refs[names.index((step, 1))][rows, :]
        upward = place[0] == (0 if step == 1 else 1)
        return jnp.where(upward if distance > 0 else jnp.logical_not(upward), first, second)

    return read


def product_at(refs, names, place, pair, rows):
    first, second = pair
    if first == -second != 0:
        return refs[names.index((second, 0))][rows, :] * refs[names.index((second, 1))][rows, :]
    read = orbital_at(refs, names, place, rows)
    value = read(first)
    return value * (value if first == second else read(second))


def views(refs, place):
    if len(refs) > 1:
        return refs
    return [refs[0].at[place[1] ^ step] for step in STEPS]


def spread_kernel(pairs, names, place, *refs):
    orbitals, (lines, columns), outs = refs[: len(names)], refs[len(names) : len(names) + 2], refs[len(names) + 2 : -1]
    outs, work = views(outs, place), refs[-1]
    lane = lane_index(GROUPS)
    for index, pair in enumerate(pairs):

        def load(tile, pair=pair):
            return product_at(orbitals, names, place, pair, pl.ds(tile, GROUPS, stride=9))

        def store(line, value, index=index):
            work[pl.ds(index * LINES + line, GROUPS, stride=16), :] = value

        unpack(16, load, store, lane)
    line_passes(work, lines, len(pairs))
    column_passes(work, columns, len(pairs))
    lane = lane_index(PLANES)
    for index in range(len(pairs)):
        for out, step in zip(outs, STEPS):
            first = (place[1] ^ step) * PLANES + index * LINES

            def load(line, first=first):
                return work[pl.ds(first + line, PLANES, stride=G), :]

            def store(tile, value, start=index * PAIR_ROWS, out=out):
                out[start + tile * PLANES : start + (tile + 1) * PLANES, :] = value

            pack(PLANES, load, store, lane)
            start = index * PAIR_ROWS + TILES * PLANES
            out[start : start + 2, :] = jnp.zeros((2, LANES), jnp.float32)


def pencil_kernel(count, parts, place, *refs):
    chunks, (kernel, forward, backward), outs = refs[:parts], refs[parts : parts + 3], refs[parts + 3 :]
    chunks = views(chunks, place)
    forward, backward = forward.at[place[1]], backward.at[place[1]]
    lane = lane_index(G)
    energies = [jnp.zeros((G, LANES), jnp.float32) for _ in range(count)]
    places = [(pair, tile) for tile in range(TILES) for pair in range(count)]
    for group in range(0, len(places), 2):
        now = places[group : group + 2]
        values = []
        for pair, tile in now:
            start = pair * PAIR_ROWS + tile * PLANES
            values.append(jnp.concatenate([chunk[start : start + PLANES, :] for chunk in chunks], axis=0))
        solved = []
        for (pair, tile), spectral in zip(now, along_columns(values, forward[...])):
            spectral = spectral[:G]
            solved.append(spectral * kernel[:, tile * LANES : (tile + 1) * LANES])
            if tile == TILES - 1:
                spectral = jnp.where(lane < PLANES * G - tile * LANES, spectral, 0.0)
            energies[pair] = energies[pair] + spectral * solved[-1]
        for (pair, tile), value in zip(now, along_columns(solved, backward[...])):
            start = pair * PAIR_ROWS + tile * PLANES
            for index, out in enumerate(outs):
                out[start : start + PLANES, :] = value[index * STEP : index * STEP + PLANES]
    for pair in range(count):
        total = jnp.full((2, LANES), jnp.sum(energies[pair]), jnp.float32)
        start = pair * PAIR_ROWS + TILES * PLANES
        for out in outs:
            out[start : start + 2, :] = total


def gather_kernel(count, parts, names, shares, place, *refs):
    chunks, (lines, columns), refs = views(refs[:parts], place), refs[parts : parts + 2], refs[parts + 2 :]
    orbitals = refs[: len(names)]
    outs, work = refs[-1 - len(shares) : -1], refs[-1]
    outs = dict(zip(shares, outs))
    added = dict(zip((2, -2), refs[len(names) : -1 - len(shares)]))
    upward = place[0] == 0
    lane = lane_index(PLANES)
    for pair in range(count):
        for chunk, step in zip(chunks, STEPS):
            first = pair * LINES + (place[1] ^ step) * PLANES

            def load(tile, start=pair * PAIR_ROWS, chunk=chunk):
                return chunk[start + tile * PLANES : start + (tile + 1) * PLANES, :]

            def store(line, value, first=first):
                work[pl.ds(first + line, PLANES, stride=G), :] = value

            unpack(PLANES, load, store, lane)
    column_passes(work, columns, count)
    line_passes(work, lines, count)
    lane = lane_index(GROUPS)

    def write(rows, terms, begun):
        shape = next(iter(terms.values())).shape
        for name in (1, 2):
            if name in terms or -name in terms:
                ahead = terms.get(name, jnp.zeros(shape, jnp.float32))
                behind = terms.get(-name, jnp.zeros(shape, jnp.float32))
                terms[name] = jnp.where(upward, ahead, behind)
                terms[-name] = jnp.where(upward, behind, ahead)
        for name, term in terms.items():
            if name in begun:
                term = term + outs[name][rows, :]
            elif name in added:
                term = term + added[name][rows, :]
            outs[name][rows, :] = term
        return set(terms)

    begun = set()
    for pair in range(count):

        def load(line, start=pair * LINES):
            return work[pl.ds(start + line, GROUPS, stride=16), :]

        written = set()

        def store(tile, value, pair=pair, written=written):
            rows = pl.ds(tile, GROUPS, stride=9)
            read = orbital_at(orbitals, names, place, rows)
            terms = {}
            for name, share in shares.items():
                for other, distance in share:
                    if other == pair:
                        terms[name] = value * read(distance)
            written |= write(rows, terms, begun)

        pack(16, load, store, lane)
        begun |= written
    totals = {}
    for name, share in shares.items():
        total = jnp.zeros((1, LANES), jnp.float32)
        for pair, _ in share:
            start = pair * PAIR_ROWS + TILES * PLANES
            for device in range(DEVICES):
                total = total + device_row(chunks, place, device, start)
        totals[name] = jnp.broadcast_to(total, (PAD_ROWS - ROWS, LANES))
    write(slice(ROWS, PAD_ROWS), totals, set())


def enter_kernel(cells, out):
    whole = ROWS // 8 * 8
    for row in range(0, whole, 8):
        out[row : row + 8, :] = cells[:, row * LANES : (row + 8) * LANES].reshape(8, LANES)
    out[whole:ROWS, :] = cells[:, whole * LANES :]
    out[ROWS:, :] = jnp.ones((PAD_ROWS - ROWS, LANES), jnp.float32)


def leave_kernel(own, *refs):
    parts, (residual, intersection) = refs[:-2], refs[-2:]

    def exchange(rows):
        return -FRACTION * sum(part[rows, :] for part in parts)

    mean = exchange(slice(ROWS, ROWS + 1)) * (1.0 / CELLS)
    intersection[...] = mean[:, :1]
    whole = ROWS // 8 * 8
    for row in range(0, whole, 8):
        rows = slice(row, row + 8)
        value = exchange(rows) - mean * own[rows, :]
        residual[:, row * LANES : (row + 8) * LANES] = value.reshape(1, 8 * LANES)
    rows = slice(whole, ROWS)
    residual[:, whole * LANES :] = exchange(rows) - mean * own[rows, :]


VMEM = pl.BlockSpec(memory_space=pltpu.VMEM)
SMEM = pl.BlockSpec(memory_space=pltpu.SMEM)
PARAMS = pltpu.CompilerParams(vmem_limit_bytes=8 * 1024 * 1024)


def chunks_of(count, parts):
    rows = count * PAIR_ROWS
    if parts == 1:
        return [jax.ShapeDtypeStruct((DEVICES, rows, LANES), jnp.float32)]
    return [jax.ShapeDtypeStruct((rows, LANES), jnp.float32)] * parts


def work_of(count):
    return [pltpu.VMEM((count * LINES, LANES), jnp.float32)]


def spread_pairs(orbitals, pairs, tables, parts=DEVICES):
    return pl.pallas_call(
        lambda *refs: spread_kernel(pairs, list(orbitals), *refs),
        out_shape=chunks_of(len(pairs), parts),
        in_specs=[SMEM] + [VMEM] * (len(orbitals) + 2),
        out_specs=[VMEM] * parts,
        scratch_shapes=work_of(len(pairs)),
        compiler_params=PARAMS,
        name="spread",
    )(tables["place"], *orbitals.values(), tables["lines"], tables["columns"])


def solve_pencils(chunks, count, tables):
    parts = len(chunks)
    return pl.pallas_call(
        lambda *refs: pencil_kernel(count, parts, *refs),
        out_shape=chunks_of(count, DEVICES),
        in_specs=[SMEM] + [VMEM] * (parts + 3),
        out_specs=[VMEM] * DEVICES,
        compiler_params=PARAMS,
        name="pencils",
    )(tables["place"], *chunks, tables["kernel"], tables["forward"], tables["backward"])


def gather_shares(chunks, count, orbitals, shares, tables, added=()):
    parts = len(chunks)
    return pl.pallas_call(
        lambda *refs: gather_kernel(count, parts, list(orbitals), shares, *refs),
        out_shape=[jax.ShapeDtypeStruct((PAD_ROWS, LANES), jnp.float32)] * len(shares),
        in_specs=[SMEM] + [VMEM] * (parts + 2 + len(orbitals) + len(added)),
        out_specs=[VMEM] * len(shares),
        scratch_shapes=work_of(count),
        compiler_params=PARAMS,
        name="gather",
    )(tables["place"], *chunks, tables["lines"], tables["columns"], *orbitals.values(), *added)


def enter(cells):
    return pl.pallas_call(
        enter_kernel,
        out_shape=jax.ShapeDtypeStruct((PAD_ROWS, LANES), jnp.float32),
        in_specs=[VMEM],
        out_specs=VMEM,
        compiler_params=PARAMS,
        name="enter",
    )(cells)


def leave(own, *parts):
    return pl.pallas_call(
        leave_kernel,
        out_shape=[jax.ShapeDtypeStruct((1, ROWS * LANES), jnp.float32), jax.ShapeDtypeStruct((1, 1), jnp.float32)],
        in_specs=[VMEM] * (1 + len(parts)),
        out_specs=[VMEM] * 2,
        compiler_params=PARAMS,
        name="leave",
    )(own, *parts)


def exchanged(chunks):
    if len(chunks) == 1:
        return [lax.all_to_all(chunks[0], "grid", split_axis=0, concat_axis=0)]
    received = [chunks[0]]
    for chunk, step in zip(chunks[1:], STEPS[1:]):
        pairs = [(device, device ^ step) for device in range(DEVICES)]
        received.append(lax.ppermute(chunk, "grid", pairs))
    return received


def after(values, *others):
    return lax.optimization_barrier((values, others))[0]


def swapped(value, step, phase):
    count = lax.axis_size("orb")
    pairs = []
    for source in range(count):
        upward = source // step % 2 == phase
        pairs.append((source, (source + (step if upward else -step)) % count))
    return lax.ppermute(value, "orb", pairs)


def shards(orbitals):
    device = lax.axis_index("grid")
    block = lax.axis_index("orb")
    tables = {
        "place": jnp.stack([block % 2, device]).astype(jnp.int32),
        "kernel": screened(device),
        "lines": jnp.asarray(line_weights()),
        "columns": jnp.asarray(column_weights()),
        "forward": jnp.asarray(np.stack([forward_weights(d) for d in range(DEVICES)])),
        "backward": jnp.asarray(np.stack([backward_weights(d) for d in range(DEVICES)])),
    }
    own = enter(orbitals)
    second = swapped(own, 1, 1)
    first = swapped(own, 1, 0)
    third = swapped(first, 1, 1)
    fourth = swapped(second, 1, 0)
    close = {0: own, (1, 0): first, (1, 1): second}
    near = spread_pairs(close, [(0, 1), (-1, 1)], tables)
    third, fourth = after((third, fourth), near)
    wide = {(1, 0): first, (1, 1): second, (2, 0): third, (2, 1): fourth}
    far = spread_pairs(wide, [(-1, 2), (-2, 2)], tables)
    none = spread_pairs({0: after(own, far)}, [(0, 0)], tables)
    near = solve_pencils(exchanged(near), 2, tables)
    far = solve_pencils(after(exchanged(far), near, none), 2, tables)
    near = exchanged(near)
    far = exchanged(far)
    shares = {1: [(0, 0), (1, -1)], -1: [(1, 1)], 0: [(0, 1)]}
    three, four, kept = gather_shares(near, 2, close, shares, tables)
    none = exchanged(after(none, kept))
    far = after(far, kept)
    shares = {1: [(0, -1), (1, -2)], -1: [(1, 2)], 2: [], -2: [(0, 2)]}
    one, two, three, four = gather_shares(far, 2, wide, shares, tables, [three, four])
    one = swapped(after(one, none), 1, 0)
    two = swapped(two, 1, 1)
    none = solve_pencils(none, 1, tables)
    four = swapped(one + four, 1, 1)
    three = swapped(two + after(three, none), 1, 0)
    none = exchanged(none)
    kept = kept + four
    (self_share,) = gather_shares(none, 1, {0: own}, {0: [(0, 0)]}, tables)
    residual, intersection = leave(own, self_share, kept, three)
    return residual, intersection.reshape(1, 1, 1)


def solution(mesh):
    in_specs = (P("orb", "grid"),)
    out_specs = (P("orb", "grid"), P("orb", None, None))
    return jax.shard_map(shards, mesh=mesh, in_specs=in_specs, out_specs=out_specs, check_vma=False)
```

```python
import math

import jax
import jax.numpy as jnp
import numpy as np
from jax import lax
from jax.experimental import pallas as pl
from jax.experimental.pallas import tpu as pltpu
from jax.sharding import PartitionSpec as P

G = 72
LANES = 128
DEVICES = 4
STEPS = (0, 2, 3, 1)
PLANES = G // DEVICES
LINES = PLANES * G
ROWS = LINES * G // LANES
PAD_ROWS = 736
GROUPS = ROWS // 9
TILES = 11
PAIR_ROWS = 200
STEP = 24
DEPTH = 80
SCREENING = 0.09
FRACTION = 0.25
CELLS = float(G * G * G)


def hartley_halves():
    indices = np.arange(G)
    phases = 2.0 * np.pi * (indices[:, None] * indices[None, :] % G) / G
    table = np.cos(phases) + np.sin(phases)
    high = table.astype(jnp.bfloat16)
    low = (table - high.astype(np.float64)).astype(jnp.bfloat16)
    return high, low


def line_weights():
    high, low = hartley_halves()
    weights = np.zeros((2 * LANES, 2 * LANES), jnp.bfloat16)
    weights[:G, :G] = high
    weights[:G, LANES : LANES + G] = low
    weights[LANES : LANES + G, :G] = high
    return weights


def stacked(left):
    gap = np.zeros((left[0].shape[0], DEPTH - G), jnp.bfloat16)
    high, low = left
    return np.concatenate([high, gap, low, gap, high, gap], axis=1)


def padded(table, rows):
    return np.concatenate([table, np.zeros((rows - table.shape[0], table.shape[1]), table.dtype)], axis=0)


def column_weights():
    return padded(stacked(hartley_halves()), DEPTH)


def in_order(table, device):
    blocks = np.split(table, DEVICES, axis=1)
    return [blocks[device ^ step] for step in STEPS]


def forward_weights(device):
    halves_in_order = [np.concatenate(in_order(half, device), axis=1) for half in hartley_halves()]
    return padded(stacked(halves_in_order), DEPTH)


def backward_weights(device):
    spread = []
    for half in hartley_halves():
        spread.append(np.concatenate([padded(block.T, STEP) for block in in_order(half, device)], axis=0))
    return stacked(spread)


def wavenumber(indices):
    return jnp.minimum(indices, G - indices).astype(jnp.float32) * (2.0 * math.pi / G)


def screened(device):
    lanes = jnp.arange(TILES * LANES, dtype=jnp.int32)
    first = wavenumber(jnp.arange(G, dtype=jnp.int32))
    second = wavenumber(jnp.minimum(device * PLANES + lanes // G, G - 1))
    third = wavenumber(lanes % G)
    squared = first[:, None] ** 2 + (second**2)[None, :] + (third**2)[None, :]
    scaled = squared / (4.0 * SCREENING * SCREENING)
    guarded = jnp.where(scaled > 0, scaled, 1.0)
    return jnp.where(scaled > 0, (1.0 - jnp.exp(-guarded)) / guarded, 1.0) / CELLS


def halves(value):
    high = value.astype(jnp.bfloat16)
    return high, (value - high.astype(jnp.float32)).astype(jnp.bfloat16)


def product(left, right):
    return jnp.dot(left, right, preferred_element_type=jnp.float32)


def along_lines(value, weights):
    result = product(jnp.concatenate(halves(value), axis=1), weights)
    return result[:, :LANES] + result[:, LANES:]


def along_columns(values, weights):
    value = jnp.concatenate(values, axis=1) if len(values) > 1 else values[0]
    value = jnp.concatenate([value, jnp.zeros((DEPTH - G, value.shape[1]), jnp.float32)], axis=0)
    high, low = halves(value)
    result = product(weights, jnp.concatenate([high, high, low], axis=0))
    return [result[:, index * LANES : (index + 1) * LANES] for index in range(len(values))]


def unpack(lines, load, store, lane):
    tiles = {}

    def tile_at(tile):
        if tile not in tiles:
            tiles.pop(tile - 2, None)
            tiles[tile] = load(tile)
        return tiles[tile]

    for line in range(lines):
        tile, shift = divmod(line * G, LANES)
        value = tile_at(tile)
        if shift:
            value = pltpu.roll(value, LANES - shift, 1)
        if shift + G > LANES:
            tail = pltpu.roll(tile_at(tile + 1), LANES - shift, 1)
            value = jnp.where(lane < LANES - shift, value, tail)
        store(line, jnp.where(lane < G, value, 0.0))


def pack(lines, load, store, lane):
    filled = jnp.zeros(lane.shape, jnp.float32)
    for line in range(lines):
        tile, shift = divmod(line * G, LANES)
        value = load(line)
        if shift:
            value = pltpu.roll(value, shift, 1)
        if shift + G < LANES:
            filled = filled + value
            if line == lines - 1:
                store(tile, filled)
            continue
        store(tile, filled + jnp.where(lane >= shift, value, 0.0))
        filled = jnp.where(lane < shift, value, 0.0)
        if line == lines - 1 and shift + G > LANES:
            store(tile + 1, filled)


def lane_index(rows):
    return lax.broadcasted_iota(jnp.int32, (rows, LANES), 1)


def line_passes(work, weights, count):
    rows = 6 * G

    def some_lines(index, carry):
        block = pl.ds(pl.multiple_of(index * rows, 8), rows)
        work[block, :] = along_lines(work[block, :], weights[...])
        return carry

    lax.fori_loop(0, count * LINES // rows, some_lines, 0, unroll=True)


def column_passes(work, weights, count):
    def planes(index, carry):
        blocks = [pl.ds(pl.multiple_of((2 * index + half) * G, 8), G) for half in range(2)]
        values = along_columns([work[block, :] for block in blocks], weights[...])
        for block, value in zip(blocks, values):
            work[block, :] = value[:G]
        return carry

    lax.fori_loop(0, count * PLANES // 2, planes, 0, unroll=3)


def device_row(chunks, place, device, row):
    value = chunks[0][row : row + 1, :]
    for chunk, step in zip(chunks[1:], STEPS[1:]):
        value = jnp.where(place[1] ^ step == device, chunk[row : row + 1, :], value)
    return value


def orbital_at(refs, names, place, rows):
    def read(distance):
        if distance in names:
            return refs[names.index(distance)][rows, :]
        step = abs(distance)
        first = refs[names.index((step, 0))][rows, :]
        second = refs[names.index((step, 1))][rows, :]
        upward = place[0] == (0 if step == 1 else 1)
        return jnp.where(upward if distance > 0 else jnp.logical_not(upward), first, second)

    return read


def product_at(refs, names, place, pair, rows):
    first, second = pair
    if first == -second != 0:
        return refs[names.index((second, 0))][rows, :] * refs[names.index((second, 1))][rows, :]
    read = orbital_at(refs, names, place, rows)
    value = read(first)
    return value * (value if first == second else read(second))


def views(refs, place):
    if len(refs) > 1:
        return refs
    return [refs[0].at[place[1] ^ step] for step in STEPS]


def spread_kernel(pairs, names, place, *refs):
    orbitals, (lines, columns), outs = refs[: len(names)], refs[len(names) : len(names) + 2], refs[len(names) + 2 : -1]
    outs, work = views(outs, place), refs[-1]
    lane = lane_index(GROUPS)
    for index, pair in enumerate(pairs):

        def load(tile, pair=pair):
            return product_at(orbitals, names, place, pair, pl.ds(tile, GROUPS, stride=9))

        def store(line, value, index=index):
            work[pl.ds(index * LINES + line, GROUPS, stride=16), :] = value

        unpack(16, load, store, lane)
    line_passes(work, lines, len(pairs))
    column_passes(work, columns, len(pairs))
    lane = lane_index(PLANES)
    for index in range(len(pairs)):
        for out, step in zip(outs, STEPS):
            first = (place[1] ^ step) * PLANES + index * LINES

            def load(line, first=first):
                return work[pl.ds(first + line, PLANES, stride=G), :]

            def store(tile, value, start=index * PAIR_ROWS, out=out):
                out[start + tile * PLANES : start + (tile + 1) * PLANES, :] = value

            pack(PLANES, load, store, lane)
            start = index * PAIR_ROWS + TILES * PLANES
            out[start : start + 2, :] = jnp.zeros((2, LANES), jnp.float32)


def pencil_kernel(count, parts, place, *refs):
    chunks, (kernel, forward, backward), outs = refs[:parts], refs[parts : parts + 3], refs[parts + 3 :]
    chunks = views(chunks, place)
    forward, backward = forward.at[place[1]], backward.at[place[1]]
    lane = lane_index(G)
    energies = [jnp.zeros((G, LANES), jnp.float32) for _ in range(count)]
    places = [(pair, tile) for tile in range(TILES) for pair in range(count)]
    for group in range(0, len(places), 2):
        now = places[group : group + 2]
        values = []
        for pair, tile in now:
            start = pair * PAIR_ROWS + tile * PLANES
            values.append(jnp.concatenate([chunk[start : start + PLANES, :] for chunk in chunks], axis=0))
        solved = []
        for (pair, tile), spectral in zip(now, along_columns(values, forward[...])):
            spectral = spectral[:G]
            solved.append(spectral * kernel[:, tile * LANES : (tile + 1) * LANES])
            if tile == TILES - 1:
                spectral = jnp.where(lane < PLANES * G - tile * LANES, spectral, 0.0)
            energies[pair] = energies[pair] + spectral * solved[-1]
        for (pair, tile), value in zip(now, along_columns(solved, backward[...])):
            start = pair * PAIR_ROWS + tile * PLANES
            for index, out in enumerate(outs):
                out[start : start + PLANES, :] = value[index * STEP : index * STEP + PLANES]
    for pair in range(count):
        total = jnp.full((2, LANES), jnp.sum(energies[pair]), jnp.float32)
        start = pair * PAIR_ROWS + TILES * PLANES
        for out in outs:
            out[start : start + 2, :] = total


def gather_kernel(count, parts, names, shares, place, *refs):
    chunks, (lines, columns), refs = views(refs[:parts], place), refs[parts : parts + 2], refs[parts + 2 :]
    orbitals = refs[: len(names)]
    outs, work = refs[-1 - len(shares) : -1], refs[-1]
    outs = dict(zip(shares, outs))
    added = dict(zip((2, -2), refs[len(names) : -1 - len(shares)]))
    upward = place[0] == 0
    lane = lane_index(PLANES)
    for pair in range(count):
        for chunk, step in zip(chunks, STEPS):
            first = pair * LINES + (place[1] ^ step) * PLANES

            def load(tile, start=pair * PAIR_ROWS, chunk=chunk):
                return chunk[start + tile * PLANES : start + (tile + 1) * PLANES, :]

            def store(line, value, first=first):
                work[pl.ds(first + line, PLANES, stride=G), :] = value

            unpack(PLANES, load, store, lane)
    column_passes(work, columns, count)
    line_passes(work, lines, count)
    lane = lane_index(GROUPS)

    def write(rows, terms, begun):
        shape = next(iter(terms.values())).shape
        for name in (1, 2):
            if name in terms or -name in terms:
                ahead = terms.get(name, jnp.zeros(shape, jnp.float32))
                behind = terms.get(-name, jnp.zeros(shape, jnp.float32))
                terms[name] = jnp.where(upward, ahead, behind)
                terms[-name] = jnp.where(upward, behind, ahead)
        for name, term in terms.items():
            if name in begun:
                term = term + outs[name][rows, :]
            elif name in added:
                term = term + added[name][rows, :]
            outs[name][rows, :] = term
        return set(terms)

    begun = set()
    for pair in range(count):

        def load(line, start=pair * LINES):
            return work[pl.ds(start + line, GROUPS, stride=16), :]

        written = set()

        def store(tile, value, pair=pair, written=written):
            rows = pl.ds(tile, GROUPS, stride=9)
            read = orbital_at(orbitals, names, place, rows)
            terms = {}
            for name, share in shares.items():
                for other, distance in share:
                    if other == pair:
                        terms[name] = value * read(distance)
            written |= write(rows, terms, begun)

        pack(16, load, store, lane)
        begun |= written
    totals = {}
    for name, share in shares.items():
        total = jnp.zeros((1, LANES), jnp.float32)
        for pair, _ in share:
            start = pair * PAIR_ROWS + TILES * PLANES
            for device in range(DEVICES):
                total = total + device_row(chunks, place, device, start)
        totals[name] = jnp.broadcast_to(total, (PAD_ROWS - ROWS, LANES))
    write(slice(ROWS, PAD_ROWS), totals, set())


def enter_kernel(cells, out):
    whole = ROWS // 8 * 8
    for row in range(0, whole, 8):
        out[row : row + 8, :] = cells[:, row * LANES : (row + 8) * LANES].reshape(8, LANES)
    out[whole:ROWS, :] = cells[:, whole * LANES :]
    out[ROWS:, :] = jnp.ones((PAD_ROWS - ROWS, LANES), jnp.float32)


def leave_kernel(own, *refs):
    parts, (residual, intersection) = refs[:-2], refs[-2:]

    def exchange(rows):
        return -FRACTION * sum(part[rows, :] for part in parts)

    mean = exchange(slice(ROWS, ROWS + 1)) * (1.0 / CELLS)
    intersection[...] = mean[:, :1]
    whole = ROWS // 8 * 8
    for row in range(0, whole, 8):
        rows = slice(row, row + 8)
        value = exchange(rows) - mean * own[rows, :]
        residual[:, row * LANES : (row + 8) * LANES] = value.reshape(1, 8 * LANES)
    rows = slice(whole, ROWS)
    residual[:, whole * LANES :] = exchange(rows) - mean * own[rows, :]


VMEM = pl.BlockSpec(memory_space=pltpu.VMEM)
SMEM = pl.BlockSpec(memory_space=pltpu.SMEM)
PARAMS = pltpu.CompilerParams(vmem_limit_bytes=8 * 1024 * 1024)


def chunks_of(count, parts):
    rows = count * PAIR_ROWS
    if parts == 1:
        return [jax.ShapeDtypeStruct((DEVICES, rows, LANES), jnp.float32)]
    return [jax.ShapeDtypeStruct((rows, LANES), jnp.float32)] * parts


def work_of(count):
    return [pltpu.VMEM((count * LINES, LANES), jnp.float32)]


def spread_pairs(orbitals, pairs, tables, parts=DEVICES):
    return pl.pallas_call(
        lambda *refs: spread_kernel(pairs, list(orbitals), *refs),
        out_shape=chunks_of(len(pairs), parts),
        in_specs=[SMEM] + [VMEM] * (len(orbitals) + 2),
        out_specs=[VMEM] * parts,
        scratch_shapes=work_of(len(pairs)),
        compiler_params=PARAMS,
        name="spread",
    )(tables["place"], *orbitals.values(), tables["lines"], tables["columns"])


def solve_pencils(chunks, count, tables):
    parts = len(chunks)
    return pl.pallas_call(
        lambda *refs: pencil_kernel(count, parts, *refs),
        out_shape=chunks_of(count, DEVICES),
        in_specs=[SMEM] + [VMEM] * (parts + 3),
        out_specs=[VMEM] * DEVICES,
        compiler_params=PARAMS,
        name="pencils",
    )(tables["place"], *chunks, tables["kernel"], tables["forward"], tables["backward"])


def gather_shares(chunks, count, orbitals, shares, tables, added=()):
    parts = len(chunks)
    return pl.pallas_call(
        lambda *refs: gather_kernel(count, parts, list(orbitals), shares, *refs),
        out_shape=[jax.ShapeDtypeStruct((PAD_ROWS, LANES), jnp.float32)] * len(shares),
        in_specs=[SMEM] + [VMEM] * (parts + 2 + len(orbitals) + len(added)),
        out_specs=[VMEM] * len(shares),
        scratch_shapes=work_of(count),
        compiler_params=PARAMS,
        name="gather",
    )(tables["place"], *chunks, tables["lines"], tables["columns"], *orbitals.values(), *added)


def enter(cells):
    return pl.pallas_call(
        enter_kernel,
        out_shape=jax.ShapeDtypeStruct((PAD_ROWS, LANES), jnp.float32),
        in_specs=[VMEM],
        out_specs=VMEM,
        compiler_params=PARAMS,
        name="enter",
    )(cells)


def leave(own, *parts):
    return pl.pallas_call(
        leave_kernel,
        out_shape=[jax.ShapeDtypeStruct((1, ROWS * LANES), jnp.float32), jax.ShapeDtypeStruct((1, 1), jnp.float32)],
        in_specs=[VMEM] * (1 + len(parts)),
        out_specs=[VMEM] * 2,
        compiler_params=PARAMS,
        name="leave",
    )(own, *parts)


def exchanged(chunks):
    if len(chunks) == 1:
        return [lax.all_to_all(chunks[0], "grid", split_axis=0, concat_axis=0)]
    received = [chunks[0]]
    for chunk, step in zip(chunks[1:], STEPS[1:]):
        pairs = [(device, device ^ step) for device in range(DEVICES)]
        received.append(lax.ppermute(chunk, "grid", pairs))
    return received


def after(values, *others):
    return lax.optimization_barrier((values, others))[0]


def swapped(value, step, phase):
    count = lax.axis_size("orb")
    pairs = []
    for source in range(count):
        upward = source // step % 2 == phase
        pairs.append((source, (source + (step if upward else -step)) % count))
    return lax.ppermute(value, "orb", pairs)


def shards(orbitals):
    device = lax.axis_index("grid")
    block = lax.axis_index("orb")
    tables = {
        "place": jnp.stack([block % 2, device]).astype(jnp.int32),
        "kernel": screened(device),
        "lines": jnp.asarray(line_weights()),
        "columns": jnp.asarray(column_weights()),
        "forward": jnp.asarray(np.stack([forward_weights(d) for d in range(DEVICES)])),
        "backward": jnp.asarray(np.stack([backward_weights(d) for d in range(DEVICES)])),
    }
    own = enter(orbitals)
    second = swapped(own, 1, 1)
    first = swapped(own, 1, 0)
    third = swapped(first, 1, 1)
    fourth = swapped(second, 1, 0)
    close = {0: own, (1, 0): first, (1, 1): second}
    near = spread_pairs(close, [(0, 1), (-1, 1)], tables)
    third, fourth = after((third, fourth), near)
    wide = {(1, 0): first, (1, 1): second, (2, 0): third, (2, 1): fourth}
    far = spread_pairs(wide, [(-1, 2), (-2, 2)], tables)
    none = spread_pairs({0: after(own, far)}, [(0, 0)], tables)
    near = solve_pencils(exchanged(near), 2, tables)
    far = solve_pencils(after(exchanged(far), near, none), 2, tables)
    near = exchanged(near)
    far = exchanged(far)
    shares = {1: [(0, 0), (1, -1)], -1: [(1, 1)], 0: [(0, 1)]}
    three, four, kept = gather_shares(near, 2, close, shares, tables)
    none = exchanged(after(none, kept))
    far = after(far, kept)
    shares = {1: [(0, -1), (1, -2)], -1: [(1, 2)], 2: [], -2: [(0, 2)]}
    one, two, three, four = gather_shares(far, 2, wide, shares, tables, [three, four])
    one = swapped(after(one, none), 1, 0)
    two = swapped(two, 1, 1)
    none = solve_pencils(none, 1, tables)
    none = exchanged(after(none, one))
    four = swapped(one + four, 1, 1)
    three = swapped(two + after(three, none), 1, 0)
    kept = kept + four
    (self_share,) = gather_shares(none, 1, {0: own}, {0: [(0, 0)]}, tables)
    residual, intersection = leave(own, self_share, kept, three)
    return residual, intersection.reshape(1, 1, 1)


def solution(mesh):
    in_specs = (P("orb", "grid"),)
    out_specs = (P("orb", "grid"), P("orb", None, None))
    return jax.shard_map(shards, mesh=mesh, in_specs=in_specs, out_specs=out_specs, check_vma=False)
```

```python
import math

import jax
import jax.numpy as jnp
import numpy as np
from jax import lax
from jax.experimental import pallas as pl
from jax.experimental.pallas import tpu as pltpu
from jax.sharding import PartitionSpec as P

G = 72
LANES = 128
DEVICES = 4
STEPS = (0, 2, 3, 1)
PLANES = G // DEVICES
LINES = PLANES * G
ROWS = LINES * G // LANES
PAD_ROWS = 736
GROUPS = ROWS // 9
TILES = {1: 11, 2: 21}
CHUNK_ROWS = {1: 200, 2: 384}
STEP = 24
DEPTH = 80
SCREENING = 0.09
FRACTION = 0.25
CELLS = float(G * G * G)


def hartley_halves():
    indices = np.arange(G)
    phases = 2.0 * np.pi * (indices[:, None] * indices[None, :] % G) / G
    table = np.cos(phases) + np.sin(phases)
    high = table.astype(jnp.bfloat16)
    low = (table - high.astype(np.float64)).astype(jnp.bfloat16)
    return high, low


def line_weights():
    high, low = hartley_halves()
    weights = np.zeros((2 * LANES, 2 * LANES), jnp.bfloat16)
    weights[:G, :G] = high
    weights[:G, LANES : LANES + G] = low
    weights[LANES : LANES + G, :G] = high
    return weights


def stacked(left):
    gap = np.zeros((left[0].shape[0], DEPTH - G), jnp.bfloat16)
    high, low = left
    return np.concatenate([high, gap, low, gap, high, gap], axis=1)


def padded(table, rows):
    return np.concatenate([table, np.zeros((rows - table.shape[0], table.shape[1]), table.dtype)], axis=0)


def column_weights():
    return padded(stacked(hartley_halves()), DEPTH)


def in_order(table, device):
    blocks = np.split(table, DEVICES, axis=1)
    return [blocks[device ^ step] for step in STEPS]


def forward_weights(device):
    halves_in_order = [np.concatenate(in_order(half, device), axis=1) for half in hartley_halves()]
    return padded(stacked(halves_in_order), DEPTH)


def backward_weights(device):
    spread = []
    for half in hartley_halves():
        spread.append(np.concatenate([padded(block.T, STEP) for block in in_order(half, device)], axis=0))
    return stacked(spread)


def wavenumber(indices):
    return jnp.minimum(indices, G - indices).astype(jnp.float32) * (2.0 * math.pi / G)


def screened(device):
    lanes = jnp.arange(TILES[2] * LANES, dtype=jnp.int32)
    first = wavenumber(jnp.arange(G, dtype=jnp.int32))
    second = wavenumber(device * PLANES + lanes // G % PLANES)
    third = wavenumber(lanes % G)
    squared = first[:, None] ** 2 + (second**2)[None, :] + (third**2)[None, :]
    scaled = squared / (4.0 * SCREENING * SCREENING)
    guarded = jnp.where(scaled > 0, scaled, 1.0)
    return jnp.where(scaled > 0, (1.0 - jnp.exp(-guarded)) / guarded, 1.0) / CELLS


def halves(value):
    high = value.astype(jnp.bfloat16)
    return high, (value - high.astype(jnp.float32)).astype(jnp.bfloat16)


def product(left, right):
    return jnp.dot(left, right, preferred_element_type=jnp.float32)


def along_lines(value, weights):
    result = product(jnp.concatenate(halves(value), axis=1), weights)
    return result[:, :LANES] + result[:, LANES:]


def along_columns(values, weights):
    value = jnp.concatenate(values, axis=1) if len(values) > 1 else values[0]
    value = jnp.concatenate([value, jnp.zeros((DEPTH - G, value.shape[1]), jnp.float32)], axis=0)
    high, low = halves(value)
    result = product(weights, jnp.concatenate([high, high, low], axis=0))
    return [result[:, index * LANES : (index + 1) * LANES] for index in range(len(values))]


def unpack(lines, load, store, lane):
    tiles = {}

    def tile_at(tile):
        if tile not in tiles:
            tiles.pop(tile - 2, None)
            tiles[tile] = load(tile)
        return tiles[tile]

    for line in range(lines):
        tile, shift = divmod(line * G, LANES)
        value = tile_at(tile)
        if shift:
            value = pltpu.roll(value, LANES - shift, 1)
        if shift + G > LANES:
            tail = pltpu.roll(tile_at(tile + 1), LANES - shift, 1)
            value = jnp.where(lane < LANES - shift, value, tail)
        store(line, jnp.where(lane < G, value, 0.0))


def pack(lines, load, store, lane):
    filled = jnp.zeros(lane.shape, jnp.float32)
    for line in range(lines):
        tile, shift = divmod(line * G, LANES)
        value = load(line)
        if shift:
            value = pltpu.roll(value, shift, 1)
        if shift + G < LANES:
            filled = filled + value
            if line == lines - 1:
                store(tile, filled)
            continue
        store(tile, filled + jnp.where(lane >= shift, value, 0.0))
        filled = jnp.where(lane < shift, value, 0.0)
        if line == lines - 1 and shift + G > LANES:
            store(tile + 1, filled)


def lane_index(rows):
    return lax.broadcasted_iota(jnp.int32, (rows, LANES), 1)


def line_passes(work, weights, count):
    rows = 6 * G

    def some_lines(index, carry):
        block = pl.ds(pl.multiple_of(index * rows, 8), rows)
        work[block, :] = along_lines(work[block, :], weights[...])
        return carry

    lax.fori_loop(0, count * LINES // rows, some_lines, 0, unroll=True)


def column_passes(work, weights, count):
    def planes(index, carry):
        blocks = [pl.ds(pl.multiple_of((2 * index + half) * G, 8), G) for half in range(2)]
        values = along_columns([work[block, :] for block in blocks], weights[...])
        for block, value in zip(blocks, values):
            work[block, :] = value[:G]
        return carry

    lax.fori_loop(0, count * PLANES // 2, planes, 0, unroll=3)


def device_row(chunks, place, device, row):
    value = chunks[0][row : row + 1, :]
    for chunk, step in zip(chunks[1:], STEPS[1:]):
        value = jnp.where(place[1] ^ step == device, chunk[row : row + 1, :], value)
    return value


def orbital_at(refs, names, place, rows):
    def read(distance):
        if distance in names:
            return refs[names.index(distance)][rows, :]
        step = abs(distance)
        first = refs[names.index((step, 0))][rows, :]
        second = refs[names.index((step, 1))][rows, :]
        upward = place[0] == (0 if step == 1 else 1)
        return jnp.where(upward if distance > 0 else jnp.logical_not(upward), first, second)

    return read


def product_at(refs, names, place, pair, rows):
    first, second = pair
    if first == -second != 0:
        return refs[names.index((second, 0))][rows, :] * refs[names.index((second, 1))][rows, :]
    read = orbital_at(refs, names, place, rows)
    value = read(first)
    return value * (value if first == second else read(second))


def views(refs, place):
    if len(refs) > 1:
        return refs
    return [refs[0].at[place[1] ^ step] for step in STEPS]


def spread_kernel(pairs, names, place, *refs):
    orbitals, (lines, columns), outs = refs[: len(names)], refs[len(names) : len(names) + 2], refs[len(names) + 2 : -1]
    outs, work = views(outs, place), refs[-1]
    lane = lane_index(GROUPS)
    for index, pair in enumerate(pairs):

        def load(tile, pair=pair):
            return product_at(orbitals, names, place, pair, pl.ds(tile, GROUPS, stride=9))

        def store(line, value, index=index):
            work[pl.ds(index * LINES + line, GROUPS, stride=16), :] = value

        unpack(16, load, store, lane)
    line_passes(work, lines, len(pairs))
    column_passes(work, columns, len(pairs))
    lane = lane_index(PLANES)
    for out, step in zip(outs, STEPS):
        first = (place[1] ^ step) * PLANES

        def load(line, first=first):
            return work[pl.ds(line // PLANES * LINES + first + line % PLANES, PLANES, stride=G), :]

        def store(tile, value, out=out):
            out[tile * PLANES : (tile + 1) * PLANES, :] = value

        pack(len(pairs) * PLANES, load, store, lane)
        start = TILES[len(pairs)] * PLANES
        out[start:, :] = jnp.zeros((CHUNK_ROWS[len(pairs)] - start, LANES), jnp.float32)


def pencil_kernel(count, parts, place, *refs):
    chunks, (kernel, forward, backward), outs = refs[:parts], refs[parts : parts + 3], refs[parts + 3 :]
    chunks = views(chunks, place)
    forward, backward = forward.at[place[1]], backward.at[place[1]]
    lane = lane_index(G)
    energies = [jnp.zeros((G, LANES), jnp.float32) for _ in range(count)]
    for group in range(0, TILES[count], 2):
        tiles = range(group, min(group + 2, TILES[count]))
        values = []
        for tile in tiles:
            rows = slice(tile * PLANES, (tile + 1) * PLANES)
            values.append(jnp.concatenate([chunk[rows, :] for chunk in chunks], axis=0))
        solved = []
        for tile, spectral in zip(tiles, along_columns(values, forward[...])):
            spectral = spectral[:G]
            solved.append(spectral * kernel[:, tile * LANES : (tile + 1) * LANES])
            energy = spectral * solved[-1]
            border = PLANES * G - tile * LANES
            if border >= LANES or count == 1:
                energies[0] = energies[0] + energy
            elif border <= 0:
                energies[1] = energies[1] + energy
            else:
                energies[0] = energies[0] + jnp.where(lane < border, energy, 0.0)
                energies[1] = energies[1] + jnp.where(lane < border, 0.0, energy)
        for tile, value in zip(tiles, along_columns(solved, backward[...])):
            for index, out in enumerate(outs):
                out[tile * PLANES : (tile + 1) * PLANES, :] = value[index * STEP : index * STEP + PLANES]
    for out in outs:
        out[TILES[count] * PLANES :, :] = jnp.zeros((CHUNK_ROWS[count] - TILES[count] * PLANES, LANES), jnp.float32)
    for pair in range(count):
        total = jnp.full((1, LANES), jnp.sum(energies[pair]), jnp.float32)
        row = TILES[count] * PLANES + pair
        for out in outs:
            out[row : row + 1, :] = total


def gather_kernel(count, parts, names, shares, place, *refs):
    chunks, (lines, columns), refs = views(refs[:parts], place), refs[parts : parts + 2], refs[parts + 2 :]
    orbitals = refs[: len(names)]
    outs, work = refs[-1 - len(shares) : -1], refs[-1]
    outs = dict(zip(shares, outs))
    added = dict(zip((2, -2), refs[len(names) : -1 - len(shares)]))
    upward = place[0] == 0
    lane = lane_index(PLANES)
    for chunk, step in zip(chunks, STEPS):
        first = (place[1] ^ step) * PLANES

        def load(tile, chunk=chunk):
            return chunk[tile * PLANES : (tile + 1) * PLANES, :]

        def store(line, value, first=first):
            work[pl.ds(line // PLANES * LINES + first + line % PLANES, PLANES, stride=G), :] = value

        unpack(count * PLANES, load, store, lane)
    column_passes(work, columns, count)
    line_passes(work, lines, count)
    lane = lane_index(GROUPS)

    def write(rows, terms, begun):
        shape = next(iter(terms.values())).shape
        for name in (1, 2):
            if name in terms or -name in terms:
                ahead = terms.get(name, jnp.zeros(shape, jnp.float32))
                behind = terms.get(-name, jnp.zeros(shape, jnp.float32))
                terms[name] = jnp.where(upward, ahead, behind)
                terms[-name] = jnp.where(upward, behind, ahead)
        for name, term in terms.items():
            if name in begun:
                term = term + outs[name][rows, :]
            elif name in added:
                term = term + added[name][rows, :]
            outs[name][rows, :] = term
        return set(terms)

    begun = set()
    for pair in range(count):

        def load(line, start=pair * LINES):
            return work[pl.ds(start + line, GROUPS, stride=16), :]

        written = set()

        def store(tile, value, pair=pair, written=written):
            rows = pl.ds(tile, GROUPS, stride=9)
            read = orbital_at(orbitals, names, place, rows)
            terms = {}
            for name, share in shares.items():
                for other, distance in share:
                    if other == pair:
                        terms[name] = value * read(distance)
            written |= write(rows, terms, begun)

        pack(16, load, store, lane)
        begun |= written
    totals = {}
    for name, share in shares.items():
        total = jnp.zeros((1, LANES), jnp.float32)
        for pair, _ in share:
            start = TILES[count] * PLANES + pair
            for device in range(DEVICES):
                total = total + device_row(chunks, place, device, start)
        totals[name] = jnp.broadcast_to(total, (PAD_ROWS - ROWS, LANES))
    write(slice(ROWS, PAD_ROWS), totals, set())


def enter_kernel(cells, out):
    whole = ROWS // 8 * 8
    for row in range(0, whole, 8):
        out[row : row + 8, :] = cells[:, row * LANES : (row + 8) * LANES].reshape(8, LANES)
    out[whole:ROWS, :] = cells[:, whole * LANES :]
    out[ROWS:, :] = jnp.ones((PAD_ROWS - ROWS, LANES), jnp.float32)


def leave_kernel(own, *refs):
    parts, (residual, intersection) = refs[:-2], refs[-2:]

    def exchange(rows):
        return -FRACTION * sum(part[rows, :] for part in parts)

    mean = exchange(slice(ROWS, ROWS + 1)) * (1.0 / CELLS)
    intersection[...] = mean[:, :1]
    whole = ROWS // 8 * 8
    for row in range(0, whole, 8):
        rows = slice(row, row + 8)
        value = exchange(rows) - mean * own[rows, :]
        residual[:, row * LANES : (row + 8) * LANES] = value.reshape(1, 8 * LANES)
    rows = slice(whole, ROWS)
    residual[:, whole * LANES :] = exchange(rows) - mean * own[rows, :]


VMEM = pl.BlockSpec(memory_space=pltpu.VMEM)
SMEM = pl.BlockSpec(memory_space=pltpu.SMEM)
PARAMS = pltpu.CompilerParams(vmem_limit_bytes=8 * 1024 * 1024)


def chunks_of(count, parts):
    rows = CHUNK_ROWS[count]
    if parts == 1:
        return [jax.ShapeDtypeStruct((DEVICES, rows, LANES), jnp.float32)]
    return [jax.ShapeDtypeStruct((rows, LANES), jnp.float32)] * parts


def work_of(count):
    return [pltpu.VMEM((count * LINES, LANES), jnp.float32)]


def spread_pairs(orbitals, pairs, tables, parts=DEVICES):
    return pl.pallas_call(
        lambda *refs: spread_kernel(pairs, list(orbitals), *refs),
        out_shape=chunks_of(len(pairs), parts),
        in_specs=[SMEM] + [VMEM] * (len(orbitals) + 2),
        out_specs=[VMEM] * parts,
        scratch_shapes=work_of(len(pairs)),
        compiler_params=PARAMS,
        name="spread",
    )(tables["place"], *orbitals.values(), tables["lines"], tables["columns"])


def solve_pencils(chunks, count, tables):
    parts = len(chunks)
    return pl.pallas_call(
        lambda *refs: pencil_kernel(count, parts, *refs),
        out_shape=chunks_of(count, DEVICES),
        in_specs=[SMEM] + [VMEM] * (parts + 3),
        out_specs=[VMEM] * DEVICES,
        compiler_params=PARAMS,
        name="pencils",
    )(tables["place"], *chunks, tables["kernel"], tables["forward"], tables["backward"])


def gather_shares(chunks, count, orbitals, shares, tables, added=()):
    parts = len(chunks)
    return pl.pallas_call(
        lambda *refs: gather_kernel(count, parts, list(orbitals), shares, *refs),
        out_shape=[jax.ShapeDtypeStruct((PAD_ROWS, LANES), jnp.float32)] * len(shares),
        in_specs=[SMEM] + [VMEM] * (parts + 2 + len(orbitals) + len(added)),
        out_specs=[VMEM] * len(shares),
        scratch_shapes=work_of(count),
        compiler_params=PARAMS,
        name="gather",
    )(tables["place"], *chunks, tables["lines"], tables["columns"], *orbitals.values(), *added)


def enter(cells):
    return pl.pallas_call(
        enter_kernel,
        out_shape=jax.ShapeDtypeStruct((PAD_ROWS, LANES), jnp.float32),
        in_specs=[VMEM],
        out_specs=VMEM,
        compiler_params=PARAMS,
        name="enter",
    )(cells)


def leave(own, *parts):
    return pl.pallas_call(
        leave_kernel,
        out_shape=[jax.ShapeDtypeStruct((1, ROWS * LANES), jnp.float32), jax.ShapeDtypeStruct((1, 1), jnp.float32)],
        in_specs=[VMEM] * (1 + len(parts)),
        out_specs=[VMEM] * 2,
        compiler_params=PARAMS,
        name="leave",
    )(own, *parts)


def exchanged(chunks):
    if len(chunks) == 1:
        return [lax.all_to_all(chunks[0], "grid", split_axis=0, concat_axis=0)]
    received = [chunks[0]]
    for chunk, step in zip(chunks[1:], STEPS[1:]):
        pairs = [(device, device ^ step) for device in range(DEVICES)]
        received.append(lax.ppermute(chunk, "grid", pairs))
    return received


def after(values, *others):
    return lax.optimization_barrier((values, others))[0]


def swapped(value, step, phase):
    count = lax.axis_size("orb")
    pairs = []
    for source in range(count):
        upward = source // step % 2 == phase
        pairs.append((source, (source + (step if upward else -step)) % count))
    return lax.ppermute(value, "orb", pairs)


def shards(orbitals):
    device = lax.axis_index("grid")
    block = lax.axis_index("orb")
    tables = {
        "place": jnp.stack([block % 2, device]).astype(jnp.int32),
        "kernel": screened(device),
        "lines": jnp.asarray(line_weights()),
        "columns": jnp.asarray(column_weights()),
        "forward": jnp.asarray(np.stack([forward_weights(d) for d in range(DEVICES)])),
        "backward": jnp.asarray(np.stack([backward_weights(d) for d in range(DEVICES)])),
    }
    own = enter(orbitals)
    second = swapped(own, 1, 1)
    first = swapped(own, 1, 0)
    third = swapped(first, 1, 1)
    fourth = swapped(second, 1, 0)
    close = {0: own, (1, 0): first, (1, 1): second}
    near = spread_pairs(close, [(0, 1), (-1, 1)], tables)
    third, fourth = after((third, fourth), near)
    wide = {(1, 1): second, (1, 0): first, (2, 1): fourth, (2, 0): third}
    far = spread_pairs(wide, [(-1, 2), (-2, 2)], tables)
    none = spread_pairs({0: after(own, far)}, [(0, 0)], tables)
    near = solve_pencils(exchanged(near), 2, tables)
    far = solve_pencils(after(exchanged(far), near, none), 2, tables)
    near = exchanged(near)
    far = exchanged(far)
    shares = {1: [(0, 0), (1, -1)], -1: [(1, 1)], 0: [(0, 1)]}
    three, four, kept = gather_shares(near, 2, close, shares, tables)
    none = exchanged(after(none, kept))
    far = after(far, kept)
    shares = {1: [(0, -1), (1, -2)], -1: [(1, 2)], 2: [], -2: [(0, 2)]}
    one, two, three, four = gather_shares(far, 2, wide, shares, tables, [three, four])
    one = swapped(after(one, none), 1, 0)
    two = swapped(two, 1, 1)
    none = solve_pencils(none, 1, tables)
    none = exchanged(after(none, one))
    four = swapped(one + four, 1, 1)
    three = swapped(two + after(three, none), 1, 0)
    kept = kept + four
    (self_share,) = gather_shares(none, 1, {0: own}, {0: [(0, 0)]}, tables)
    residual, intersection = leave(own, self_share, kept, three)
    return residual, intersection.reshape(1, 1, 1)


def solution(mesh):
    in_specs = (P("orb", "grid"),)
    out_specs = (P("orb", "grid"), P("orb", None, None))
    return jax.shard_map(shards, mesh=mesh, in_specs=in_specs, out_specs=out_specs, check_vma=False)
```

```python
import math

import jax
import jax.numpy as jnp
import numpy as np
from jax import lax
from jax.experimental import pallas as pl
from jax.experimental.pallas import tpu as pltpu
from jax.sharding import PartitionSpec as P

G = 72
LANES = 128
DEVICES = 4
STEPS = (0, 2, 3, 1)
PLANES = G // DEVICES
LINES = PLANES * G
ROWS = LINES * G // LANES
PAD_ROWS = 736
GROUPS = ROWS // 9
TILES = {1: 11, 2: 21}
CHUNK_ROWS = {1: 200, 2: 384}
STEP = 24
DEPTH = 80
SCREENING = 0.09
FRACTION = 0.25
CELLS = float(G * G * G)


def hartley_halves():
    indices = np.arange(G)
    phases = 2.0 * np.pi * (indices[:, None] * indices[None, :] % G) / G
    table = np.cos(phases) + np.sin(phases)
    high = table.astype(jnp.bfloat16)
    low = (table - high.astype(np.float64)).astype(jnp.bfloat16)
    return high, low


def line_weights():
    high, low = hartley_halves()
    weights = np.zeros((2 * LANES, 2 * LANES), jnp.bfloat16)
    weights[:G, :G] = high
    weights[:G, LANES : LANES + G] = low
    weights[LANES : LANES + G, :G] = high
    return weights


def stacked(left):
    gap = np.zeros((left[0].shape[0], DEPTH - G), jnp.bfloat16)
    high, low = left
    return np.concatenate([high, gap, low, gap, high, gap], axis=1)


def padded(table, rows):
    return np.concatenate([table, np.zeros((rows - table.shape[0], table.shape[1]), table.dtype)], axis=0)


def column_weights():
    return padded(stacked(hartley_halves()), DEPTH)


def in_order(table, device):
    blocks = np.split(table, DEVICES, axis=1)
    return [blocks[device ^ step] for step in STEPS]


def forward_weights(device):
    halves_in_order = [np.concatenate(in_order(half, device), axis=1) for half in hartley_halves()]
    return padded(stacked(halves_in_order), DEPTH)


def backward_weights(device):
    spread = []
    for half in hartley_halves():
        spread.append(np.concatenate([padded(block.T, STEP) for block in in_order(half, device)], axis=0))
    return stacked(spread)


def wavenumber(indices):
    return jnp.minimum(indices, G - indices).astype(jnp.float32) * (2.0 * math.pi / G)


def screened(device):
    lanes = jnp.arange(TILES[2] * LANES, dtype=jnp.int32)
    first = wavenumber(jnp.arange(G, dtype=jnp.int32))
    second = wavenumber(device * PLANES + lanes // G % PLANES)
    third = wavenumber(lanes % G)
    squared = first[:, None] ** 2 + (second**2)[None, :] + (third**2)[None, :]
    scaled = squared / (4.0 * SCREENING * SCREENING)
    guarded = jnp.where(scaled > 0, scaled, 1.0)
    return jnp.where(scaled > 0, (1.0 - jnp.exp(-guarded)) / guarded, 1.0) / CELLS


def halves(value):
    high = value.astype(jnp.bfloat16)
    return high, (value - high.astype(jnp.float32)).astype(jnp.bfloat16)


def product(left, right):
    return jnp.dot(left, right, preferred_element_type=jnp.float32)


def along_lines(value, weights):
    result = product(jnp.concatenate(halves(value), axis=1), weights)
    return result[:, :LANES] + result[:, LANES:]


def along_columns(values, weights):
    value = jnp.concatenate(values, axis=1) if len(values) > 1 else values[0]
    value = jnp.concatenate([value, jnp.zeros((DEPTH - G, value.shape[1]), jnp.float32)], axis=0)
    high, low = halves(value)
    result = product(weights, jnp.concatenate([high, high, low], axis=0))
    return [result[:, index * LANES : (index + 1) * LANES] for index in range(len(values))]


def unpack(lines, load, store, lane):
    tiles = {}

    def tile_at(tile):
        if tile not in tiles:
            tiles.pop(tile - 2, None)
            tiles[tile] = load(tile)
        return tiles[tile]

    for line in range(lines):
        tile, shift = divmod(line * G, LANES)
        value = tile_at(tile)
        if shift:
            value = pltpu.roll(value, LANES - shift, 1)
        if shift + G > LANES:
            tail = pltpu.roll(tile_at(tile + 1), LANES - shift, 1)
            value = jnp.where(lane < LANES - shift, value, tail)
        store(line, jnp.where(lane < G, value, 0.0))


def pack(lines, load, store, lane):
    filled = jnp.zeros(lane.shape, jnp.float32)
    for line in range(lines):
        tile, shift = divmod(line * G, LANES)
        value = load(line)
        if shift:
            value = pltpu.roll(value, shift, 1)
        if shift + G < LANES:
            filled = filled + value
            if line == lines - 1:
                store(tile, filled)
            continue
        store(tile, filled + jnp.where(lane >= shift, value, 0.0))
        filled = jnp.where(lane < shift, value, 0.0)
        if line == lines - 1 and shift + G > LANES:
            store(tile + 1, filled)


def lane_index(rows):
    return lax.broadcasted_iota(jnp.int32, (rows, LANES), 1)


def line_passes(work, weights, count):
    rows = 6 * G

    def some_lines(index, carry):
        block = pl.ds(pl.multiple_of(index * rows, 8), rows)
        work[block, :] = along_lines(work[block, :], weights[...])
        return carry

    lax.fori_loop(0, count * LINES // rows, some_lines, 0, unroll=True)


def column_passes(work, weights, count):
    def planes(index, carry):
        blocks = [pl.ds(pl.multiple_of((2 * index + half) * G, 8), G) for half in range(2)]
        values = along_columns([work[block, :] for block in blocks], weights[...])
        for block, value in zip(blocks, values):
            work[block, :] = value[:G]
        return carry

    lax.fori_loop(0, count * PLANES // 2, planes, 0, unroll=3)


def device_row(chunks, place, device, row):
    value = chunks[0][row : row + 1, :]
    for chunk, step in zip(chunks[1:], STEPS[1:]):
        value = jnp.where(place[1] ^ step == device, chunk[row : row + 1, :], value)
    return value


def orbital_at(refs, names, place, rows):
    def read(distance):
        if distance in names:
            return refs[names.index(distance)][rows, :]
        step = abs(distance)
        first = refs[names.index((step, 0))][rows, :]
        second = refs[names.index((step, 1))][rows, :]
        upward = place[0] == (0 if step == 1 else 1)
        return jnp.where(upward if distance > 0 else jnp.logical_not(upward), first, second)

    return read


def product_at(refs, names, place, pair, rows):
    first, second = pair
    if first == -second != 0:
        return refs[names.index((second, 0))][rows, :] * refs[names.index((second, 1))][rows, :]
    read = orbital_at(refs, names, place, rows)
    value = read(first)
    return value * (value if first == second else read(second))


def views(refs, place):
    if len(refs) > 1:
        return refs
    return [refs[0].at[place[1] ^ step] for step in STEPS]


def spread_kernel(pairs, names, place, *refs):
    orbitals, (lines, columns), outs = refs[: len(names)], refs[len(names) : len(names) + 2], refs[len(names) + 2 : -1]
    outs, work = views(outs, place), refs[-1]
    lane = lane_index(GROUPS)
    for index, pair in enumerate(pairs):

        def load(tile, pair=pair):
            return product_at(orbitals, names, place, pair, pl.ds(tile, GROUPS, stride=9))

        def store(line, value, index=index):
            work[pl.ds(index * LINES + line, GROUPS, stride=16), :] = value

        unpack(16, load, store, lane)
    line_passes(work, lines, len(pairs))
    column_passes(work, columns, len(pairs))
    lane = lane_index(PLANES)
    for out, step in zip(outs, STEPS):
        first = (place[1] ^ step) * PLANES

        def load(line, first=first):
            return work[pl.ds(line // PLANES * LINES + first + line % PLANES, PLANES, stride=G), :]

        def store(tile, value, out=out):
            out[tile * PLANES : (tile + 1) * PLANES, :] = value

        pack(len(pairs) * PLANES, load, store, lane)
        start = TILES[len(pairs)] * PLANES
        out[start:, :] = jnp.zeros((CHUNK_ROWS[len(pairs)] - start, LANES), jnp.float32)


def pencil_kernel(count, parts, place, *refs):
    chunks, (kernel, forward, backward), outs = refs[:parts], refs[parts : parts + 3], refs[parts + 3 :]
    chunks = views(chunks, place)
    forward, backward = forward.at[place[1]], backward.at[place[1]]
    lane = lane_index(G)
    energies = [jnp.zeros((G, LANES), jnp.float32) for _ in range(count)]
    for group in range(0, TILES[count], 2):
        tiles = range(group, min(group + 2, TILES[count]))
        values = []
        for tile in tiles:
            rows = slice(tile * PLANES, (tile + 1) * PLANES)
            values.append(jnp.concatenate([chunk[rows, :] for chunk in chunks], axis=0))
        solved = []
        for tile, spectral in zip(tiles, along_columns(values, forward[...])):
            spectral = spectral[:G]
            solved.append(spectral * kernel[:, tile * LANES : (tile + 1) * LANES])
            energy = spectral * solved[-1]
            border = PLANES * G - tile * LANES
            if border >= LANES or count == 1:
                energies[0] = energies[0] + energy
            elif border <= 0:
                energies[1] = energies[1] + energy
            else:
                energies[0] = energies[0] + jnp.where(lane < border, energy, 0.0)
                energies[1] = energies[1] + jnp.where(lane < border, 0.0, energy)
        for tile, value in zip(tiles, along_columns(solved, backward[...])):
            for index, out in enumerate(outs):
                out[tile * PLANES : (tile + 1) * PLANES, :] = value[index * STEP : index * STEP + PLANES]
    for out in outs:
        out[TILES[count] * PLANES :, :] = jnp.zeros((CHUNK_ROWS[count] - TILES[count] * PLANES, LANES), jnp.float32)
    for pair in range(count):
        total = jnp.full((1, LANES), jnp.sum(energies[pair]), jnp.float32)
        row = TILES[count] * PLANES + pair
        for out in outs:
            out[row : row + 1, :] = total


def gather_kernel(count, parts, names, shares, place, *refs):
    chunks, (lines, columns), refs = views(refs[:parts], place), refs[parts : parts + 2], refs[parts + 2 :]
    orbitals = refs[: len(names)]
    outs, work = refs[-1 - len(shares) : -1], refs[-1]
    outs = dict(zip(shares, outs))
    added = dict(zip((2, -2), refs[len(names) : -1 - len(shares)]))
    upward = place[0] == 0
    lane = lane_index(PLANES)
    for chunk, step in zip(chunks, STEPS):
        first = (place[1] ^ step) * PLANES

        def load(tile, chunk=chunk):
            return chunk[tile * PLANES : (tile + 1) * PLANES, :]

        def store(line, value, first=first):
            work[pl.ds(line // PLANES * LINES + first + line % PLANES, PLANES, stride=G), :] = value

        unpack(count * PLANES, load, store, lane)
    column_passes(work, columns, count)
    line_passes(work, lines, count)
    lane = lane_index(GROUPS)

    def write(rows, terms, begun):
        shape = next(iter(terms.values())).shape
        for name in (1, 2):
            if name in terms or -name in terms:
                ahead = terms.get(name, jnp.zeros(shape, jnp.float32))
                behind = terms.get(-name, jnp.zeros(shape, jnp.float32))
                terms[name] = jnp.where(upward, ahead, behind)
                terms[-name] = jnp.where(upward, behind, ahead)
        for name, term in terms.items():
            if name in begun:
                term = term + outs[name][rows, :]
            elif name in added:
                term = term + added[name][rows, :]
            outs[name][rows, :] = term
        return set(terms)

    begun = set()
    for pair in range(count):

        def load(line, start=pair * LINES):
            return work[pl.ds(start + line, GROUPS, stride=16), :]

        written = set()

        def store(tile, value, pair=pair, written=written):
            rows = pl.ds(tile, GROUPS, stride=9)
            read = orbital_at(orbitals, names, place, rows)
            terms = {}
            for name, share in shares.items():
                for other, distance in share:
                    if other == pair:
                        terms[name] = value * read(distance)
            written |= write(rows, terms, begun)

        pack(16, load, store, lane)
        begun |= written
    totals = {}
    for name, share in shares.items():
        total = jnp.zeros((1, LANES), jnp.float32)
        for pair, _ in share:
            start = TILES[count] * PLANES + pair
            for device in range(DEVICES):
                total = total + device_row(chunks, place, device, start)
        totals[name] = jnp.broadcast_to(total, (PAD_ROWS - ROWS, LANES))
    write(slice(ROWS, PAD_ROWS), totals, set())


def enter_kernel(cells, out):
    whole = ROWS // 8 * 8
    for row in range(0, whole, 8):
        out[row : row + 8, :] = cells[:, row * LANES : (row + 8) * LANES].reshape(8, LANES)
    out[whole:ROWS, :] = cells[:, whole * LANES :]
    out[ROWS:, :] = jnp.ones((PAD_ROWS - ROWS, LANES), jnp.float32)


def leave_kernel(own, *refs):
    parts, (residual, intersection) = refs[:-2], refs[-2:]

    def exchange(rows):
        return -FRACTION * sum(part[rows, :] for part in parts)

    mean = exchange(slice(ROWS, ROWS + 1)) * (1.0 / CELLS)
    intersection[...] = mean[:, :1]
    whole = ROWS // 8 * 8
    for row in range(0, whole, 8):
        rows = slice(row, row + 8)
        value = exchange(rows) - mean * own[rows, :]
        residual[:, row * LANES : (row + 8) * LANES] = value.reshape(1, 8 * LANES)
    rows = slice(whole, ROWS)
    residual[:, whole * LANES :] = exchange(rows) - mean * own[rows, :]


VMEM = pl.BlockSpec(memory_space=pltpu.VMEM)
SMEM = pl.BlockSpec(memory_space=pltpu.SMEM)
PARAMS = pltpu.CompilerParams(vmem_limit_bytes=8 * 1024 * 1024)


def chunks_of(count, parts):
    rows = CHUNK_ROWS[count]
    if parts == 1:
        return [jax.ShapeDtypeStruct((DEVICES, rows, LANES), jnp.float32)]
    return [jax.ShapeDtypeStruct((rows, LANES), jnp.float32)] * parts


def work_of(count):
    return [pltpu.VMEM((count * LINES, LANES), jnp.float32)]


def spread_pairs(orbitals, pairs, tables, parts=DEVICES):
    return pl.pallas_call(
        lambda *refs: spread_kernel(pairs, list(orbitals), *refs),
        out_shape=chunks_of(len(pairs), parts),
        in_specs=[SMEM] + [VMEM] * (len(orbitals) + 2),
        out_specs=[VMEM] * parts,
        scratch_shapes=work_of(len(pairs)),
        compiler_params=PARAMS,
        name="spread",
    )(tables["place"], *orbitals.values(), tables["lines"], tables["columns"])


def solve_pencils(chunks, count, tables):
    parts = len(chunks)
    return pl.pallas_call(
        lambda *refs: pencil_kernel(count, parts, *refs),
        out_shape=chunks_of(count, DEVICES),
        in_specs=[SMEM] + [VMEM] * (parts + 3),
        out_specs=[VMEM] * DEVICES,
        compiler_params=PARAMS,
        name="pencils",
    )(tables["place"], *chunks, tables["kernel"], tables["forward"], tables["backward"])


def gather_shares(chunks, count, orbitals, shares, tables, added=()):
    parts = len(chunks)
    return pl.pallas_call(
        lambda *refs: gather_kernel(count, parts, list(orbitals), shares, *refs),
        out_shape=[jax.ShapeDtypeStruct((PAD_ROWS, LANES), jnp.float32)] * len(shares),
        in_specs=[SMEM] + [VMEM] * (parts + 2 + len(orbitals) + len(added)),
        out_specs=[VMEM] * len(shares),
        scratch_shapes=work_of(count),
        compiler_params=PARAMS,
        name="gather",
    )(tables["place"], *chunks, tables["lines"], tables["columns"], *orbitals.values(), *added)


def enter(cells):
    return pl.pallas_call(
        enter_kernel,
        out_shape=jax.ShapeDtypeStruct((PAD_ROWS, LANES), jnp.float32),
        in_specs=[VMEM],
        out_specs=VMEM,
        compiler_params=PARAMS,
        name="enter",
    )(cells)


def leave(own, *parts):
    return pl.pallas_call(
        leave_kernel,
        out_shape=[jax.ShapeDtypeStruct((1, ROWS * LANES), jnp.float32), jax.ShapeDtypeStruct((1, 1), jnp.float32)],
        in_specs=[VMEM] * (1 + len(parts)),
        out_specs=[VMEM] * 2,
        compiler_params=PARAMS,
        name="leave",
    )(own, *parts)


def exchanged(chunks):
    if len(chunks) == 1:
        return [lax.all_to_all(chunks[0], "grid", split_axis=0, concat_axis=0)]
    received = [chunks[0]]
    for chunk, step in zip(chunks[1:], STEPS[1:]):
        pairs = [(device, device ^ step) for device in range(DEVICES)]
        received.append(lax.ppermute(chunk, "grid", pairs))
    return received


def after(values, *others):
    return lax.optimization_barrier((values, others))[0]


def swapped(value, step, phase):
    count = lax.axis_size("orb")
    pairs = []
    for source in range(count):
        upward = source // step % 2 == phase
        pairs.append((source, (source + (step if upward else -step)) % count))
    return lax.ppermute(value, "orb", pairs)


def shards(orbitals):
    device = lax.axis_index("grid")
    block = lax.axis_index("orb")
    tables = {
        "place": jnp.stack([block % 2, device]).astype(jnp.int32),
        "kernel": screened(device),
        "lines": jnp.asarray(line_weights()),
        "columns": jnp.asarray(column_weights()),
        "forward": jnp.asarray(np.stack([forward_weights(d) for d in range(DEVICES)])),
        "backward": jnp.asarray(np.stack([backward_weights(d) for d in range(DEVICES)])),
    }
    own = enter(orbitals)
    second = swapped(own, 1, 1)
    first = swapped(own, 1, 0)
    third = swapped(first, 1, 1)
    fourth = swapped(second, 1, 0)
    close = {0: own, (1, 0): first, (1, 1): second}
    near = spread_pairs(close, [(0, 1), (-1, 1)], tables)
    third, fourth = after((third, fourth), near)
    wide = {(1, 1): second, (1, 0): first, (2, 1): fourth, (2, 0): third}
    far = spread_pairs(wide, [(-1, 2), (-2, 2)], tables)
    none = spread_pairs({0: after(own, far)}, [(0, 0)], tables)
    near = solve_pencils(exchanged(near), 2, tables)
    far = solve_pencils(after(exchanged(far), near, none), 2, tables)
    near = exchanged(near)
    far = exchanged(far)
    shares = {1: [(0, 0), (1, -1)], -1: [(1, 1)], 0: [(0, 1)]}
    three, four, kept = gather_shares(near, 2, close, shares, tables)
    none = exchanged(after(none, kept))
    far = after(far, kept)
    shares = {1: [(0, -1), (1, -2)], -1: [(1, 2)], 2: [], -2: [(0, 2)]}
    one, two, three, four = gather_shares(far, 2, wide, shares, tables, [three, four])
    one = swapped(after(one, none), 1, 0)
    two = swapped(two, 1, 1)
    none = solve_pencils(none, 1, tables)
    four = swapped(one + four, 1, 1)
    three = swapped(two + after(three, none), 1, 0)
    none = exchanged(none)
    kept = kept + four
    (self_share,) = gather_shares(none, 1, {0: own}, {0: [(0, 0)]}, tables)
    residual, intersection = leave(own, self_share, kept, three)
    return residual, intersection.reshape(1, 1, 1)


def solution(mesh):
    in_specs = (P("orb", "grid"),)
    out_specs = (P("orb", "grid"), P("orb", None, None))
    return jax.shard_map(shards, mesh=mesh, in_specs=in_specs, out_specs=out_specs, check_vma=False)
```

```python
import math

import jax
import jax.numpy as jnp
import numpy as np
from jax import lax
from jax.experimental import pallas as pl
from jax.experimental.pallas import tpu as pltpu
from jax.sharding import PartitionSpec as P

G = 72
LANES = 128
DEVICES = 4
STEPS = (0, 2, 3, 1)
PLANES = G // DEVICES
LINES = PLANES * G
ROWS = LINES * G // LANES
PAD_ROWS = 736
GROUPS = ROWS // 9
TILES = 11
PAIR_ROWS = 200
STEP = 24
DEPTH = 80
SCREENING = 0.09
FRACTION = 0.25
CELLS = float(G * G * G)


def hartley_halves():
    indices = np.arange(G)
    phases = 2.0 * np.pi * (indices[:, None] * indices[None, :] % G) / G
    table = np.cos(phases) + np.sin(phases)
    high = table.astype(jnp.bfloat16)
    low = (table - high.astype(np.float64)).astype(jnp.bfloat16)
    return high, low


def line_weights():
    high, low = hartley_halves()
    weights = np.zeros((2 * LANES, 2 * LANES), jnp.bfloat16)
    weights[:G, :G] = high
    weights[:G, LANES : LANES + G] = low
    weights[LANES : LANES + G, :G] = high
    return weights


def stacked(left):
    gap = np.zeros((left[0].shape[0], DEPTH - G), jnp.bfloat16)
    high, low = left
    return np.concatenate([high, gap, low, gap, high, gap], axis=1)


def padded(table, rows):
    return np.concatenate([table, np.zeros((rows - table.shape[0], table.shape[1]), table.dtype)], axis=0)


def column_weights():
    return padded(stacked(hartley_halves()), DEPTH)


def in_order(table, device):
    blocks = np.split(table, DEVICES, axis=1)
    return [blocks[device ^ step] for step in STEPS]


def forward_weights(device):
    halves_in_order = [np.concatenate(in_order(half, device), axis=1) for half in hartley_halves()]
    return padded(stacked(halves_in_order), DEPTH)


def backward_weights(device):
    spread = []
    for half in hartley_halves():
        spread.append(np.concatenate([padded(block.T, STEP) for block in in_order(half, device)], axis=0))
    return stacked(spread)


def wavenumber(indices):
    return jnp.minimum(indices, G - indices).astype(jnp.float32) * (2.0 * math.pi / G)


def screened(device):
    lanes = jnp.arange(TILES * LANES, dtype=jnp.int32)
    first = wavenumber(jnp.arange(G, dtype=jnp.int32))
    second = wavenumber(jnp.minimum(device * PLANES + lanes // G, G - 1))
    third = wavenumber(lanes % G)
    squared = first[:, None] ** 2 + (second**2)[None, :] + (third**2)[None, :]
    scaled = squared / (4.0 * SCREENING * SCREENING)
    guarded = jnp.where(scaled > 0, scaled, 1.0)
    return jnp.where(scaled > 0, (1.0 - jnp.exp(-guarded)) / guarded, 1.0) / CELLS


def halves(value):
    high = value.astype(jnp.bfloat16)
    return high, (value - high.astype(jnp.float32)).astype(jnp.bfloat16)


def product(left, right):
    return jnp.dot(left, right, preferred_element_type=jnp.float32)


def along_lines(value, weights):
    result = product(jnp.concatenate(halves(value), axis=1), weights)
    return result[:, :LANES] + result[:, LANES:]


def along_columns(values, weights):
    value = jnp.concatenate(values, axis=1) if len(values) > 1 else values[0]
    value = jnp.concatenate([value, jnp.zeros((DEPTH - G, value.shape[1]), jnp.float32)], axis=0)
    high, low = halves(value)
    result = product(weights, jnp.concatenate([high, high, low], axis=0))
    return [result[:, index * LANES : (index + 1) * LANES] for index in range(len(values))]


def unpack(lines, load, store, lane):
    tiles = {}

    def tile_at(tile):
        if tile not in tiles:
            tiles.pop(tile - 2, None)
            tiles[tile] = load(tile)
        return tiles[tile]

    for line in range(lines):
        tile, shift = divmod(line * G, LANES)
        value = tile_at(tile)
        if shift:
            value = pltpu.roll(value, LANES - shift, 1)
        if shift + G > LANES:
            tail = pltpu.roll(tile_at(tile + 1), LANES - shift, 1)
            value = jnp.where(lane < LANES - shift, value, tail)
        store(line, jnp.where(lane < G, value, 0.0))


def pack(lines, load, store, lane):
    filled = jnp.zeros(lane.shape, jnp.float32)
    for line in range(lines):
        tile, shift = divmod(line * G, LANES)
        value = load(line)
        if shift:
            value = pltpu.roll(value, shift, 1)
        if shift + G < LANES:
            filled = filled + value
            if line == lines - 1:
                store(tile, filled)
            continue
        store(tile, filled + jnp.where(lane >= shift, value, 0.0))
        filled = jnp.where(lane < shift, value, 0.0)
        if line == lines - 1 and shift + G > LANES:
            store(tile + 1, filled)


def lane_index(rows):
    return lax.broadcasted_iota(jnp.int32, (rows, LANES), 1)


def line_passes(work, weights, count):
    rows = 6 * G

    def some_lines(index, carry):
        block = pl.ds(pl.multiple_of(index * rows, 8), rows)
        work[block, :] = along_lines(work[block, :], weights[...])
        return carry

    lax.fori_loop(0, count * LINES // rows, some_lines, 0, unroll=True)


def column_passes(work, weights, count):
    def planes(index, carry):
        blocks = [pl.ds(pl.multiple_of((2 * index + half) * G, 8), G) for half in range(2)]
        values = along_columns([work[block, :] for block in blocks], weights[...])
        for block, value in zip(blocks, values):
            work[block, :] = value[:G]
        return carry

    lax.fori_loop(0, count * PLANES // 2, planes, 0, unroll=3)


def device_row(chunks, place, device, row):
    value = chunks[0][row : row + 1, :]
    for chunk, step in zip(chunks[1:], STEPS[1:]):
        value = jnp.where(place[1] ^ step == device, chunk[row : row + 1, :], value)
    return value


def orbital_at(refs, names, place, rows):
    def read(distance):
        if distance in names:
            return refs[names.index(distance)][rows, :]
        step = abs(distance)
        first = refs[names.index((step, 0))][rows, :]
        second = refs[names.index((step, 1))][rows, :]
        upward = place[0] == (0 if step == 1 else 1)
        return jnp.where(upward if distance > 0 else jnp.logical_not(upward), first, second)

    return read


def product_at(refs, names, place, pair, rows):
    first, second = pair
    if first == -second != 0:
        return refs[names.index((second, 0))][rows, :] * refs[names.index((second, 1))][rows, :]
    read = orbital_at(refs, names, place, rows)
    value = read(first)
    return value * (value if first == second else read(second))


def views(refs, place):
    if len(refs) > 1:
        return refs
    return [refs[0].at[place[1] ^ step] for step in STEPS]


def spread_kernel(pairs, names, place, *refs):
    orbitals, (lines, columns), outs = refs[: len(names)], refs[len(names) : len(names) + 2], refs[len(names) + 2 : -1]
    outs, work = views(outs, place), refs[-1]
    lane = lane_index(GROUPS)
    for index, pair in enumerate(pairs):

        def load(tile, pair=pair):
            return product_at(orbitals, names, place, pair, pl.ds(tile, GROUPS, stride=9))

        def store(line, value, index=index):
            work[pl.ds(index * LINES + line, GROUPS, stride=16), :] = value

        unpack(16, load, store, lane)
    line_passes(work, lines, len(pairs))
    column_passes(work, columns, len(pairs))
    lane = lane_index(PLANES)
    for index in range(len(pairs)):
        for out, step in zip(outs, STEPS):
            first = (place[1] ^ step) * PLANES + index * LINES

            def load(line, first=first):
                return work[pl.ds(first + line, PLANES, stride=G), :]

            def store(tile, value, start=index * PAIR_ROWS, out=out):
                out[start + tile * PLANES : start + (tile + 1) * PLANES, :] = value

            pack(PLANES, load, store, lane)
            start = index * PAIR_ROWS + TILES * PLANES
            out[start : start + 2, :] = jnp.zeros((2, LANES), jnp.float32)


def pencil_kernel(count, parts, place, *refs):
    chunks, (kernel, forward, backward), outs = refs[:parts], refs[parts : parts + 3], refs[parts + 3 :]
    chunks = views(chunks, place)
    forward, backward = forward.at[place[1]], backward.at[place[1]]
    lane = lane_index(G)
    energies = [jnp.zeros((G, LANES), jnp.float32) for _ in range(count)]
    places = [(pair, tile) for tile in range(TILES) for pair in range(count)]
    for group in range(0, len(places), 2):
        now = places[group : group + 2]
        values = []
        for pair, tile in now:
            start = pair * PAIR_ROWS + tile * PLANES
            values.append(jnp.concatenate([chunk[start : start + PLANES, :] for chunk in chunks], axis=0))
        solved = []
        for (pair, tile), spectral in zip(now, along_columns(values, forward[...])):
            spectral = spectral[:G]
            solved.append(spectral * kernel[:, tile * LANES : (tile + 1) * LANES])
            if tile == TILES - 1:
                spectral = jnp.where(lane < PLANES * G - tile * LANES, spectral, 0.0)
            energies[pair] = energies[pair] + spectral * solved[-1]
        for (pair, tile), value in zip(now, along_columns(solved, backward[...])):
            start = pair * PAIR_ROWS + tile * PLANES
            for index, out in enumerate(outs):
                out[start : start + PLANES, :] = value[index * STEP : index * STEP + PLANES]
    for pair in range(count):
        total = jnp.full((2, LANES), jnp.sum(energies[pair]), jnp.float32)
        start = pair * PAIR_ROWS + TILES * PLANES
        for out in outs:
            out[start : start + 2, :] = total


def gather_kernel(count, parts, names, shares, place, *refs):
    chunks, (lines, columns), refs = views(refs[:parts], place), refs[parts : parts + 2], refs[parts + 2 :]
    orbitals = refs[: len(names)]
    outs, work = refs[-1 - len(shares) : -1], refs[-1]
    outs = dict(zip(shares, outs))
    added = dict(zip((2, -2), refs[len(names) : -1 - len(shares)]))
    upward = place[0] == 0
    lane = lane_index(PLANES)
    for pair in range(count):
        for chunk, step in zip(chunks, STEPS):
            first = pair * LINES + (place[1] ^ step) * PLANES

            def load(tile, start=pair * PAIR_ROWS, chunk=chunk):
                return chunk[start + tile * PLANES : start + (tile + 1) * PLANES, :]

            def store(line, value, first=first):
                work[pl.ds(first + line, PLANES, stride=G), :] = value

            unpack(PLANES, load, store, lane)
    column_passes(work, columns, count)
    line_passes(work, lines, count)
    lane = lane_index(GROUPS)

    def write(rows, terms, begun):
        shape = next(iter(terms.values())).shape
        for name in (1, 2):
            if name in terms or -name in terms:
                ahead = terms.get(name, jnp.zeros(shape, jnp.float32))
                behind = terms.get(-name, jnp.zeros(shape, jnp.float32))
                terms[name] = jnp.where(upward, ahead, behind)
                terms[-name] = jnp.where(upward, behind, ahead)
        for name, term in terms.items():
            if name in begun:
                term = term + outs[name][rows, :]
            elif name in added:
                term = term + added[name][rows, :]
            outs[name][rows, :] = term
        return set(terms)

    begun = set()
    for pair in range(count):

        def load(line, start=pair * LINES):
            return work[pl.ds(start + line, GROUPS, stride=16), :]

        written = set()

        def store(tile, value, pair=pair, written=written):
            rows = pl.ds(tile, GROUPS, stride=9)
            read = orbital_at(orbitals, names, place, rows)
            terms = {}
            for name, share in shares.items():
                for other, distance in share:
                    if other == pair:
                        terms[name] = value * read(distance)
            written |= write(rows, terms, begun)

        pack(16, load, store, lane)
        begun |= written
    totals = {}
    for name, share in shares.items():
        total = jnp.zeros((1, LANES), jnp.float32)
        for pair, _ in share:
            start = pair * PAIR_ROWS + TILES * PLANES
            for device in range(DEVICES):
                total = total + device_row(chunks, place, device, start)
        totals[name] = jnp.broadcast_to(total, (PAD_ROWS - ROWS, LANES))
    write(slice(ROWS, PAD_ROWS), totals, set())


def enter_kernel(cells, out):
    whole = ROWS // 8 * 8
    for row in range(0, whole, 8):
        out[row : row + 8, :] = cells[:, row * LANES : (row + 8) * LANES].reshape(8, LANES)
    out[whole:ROWS, :] = cells[:, whole * LANES :]
    out[ROWS:, :] = jnp.ones((PAD_ROWS - ROWS, LANES), jnp.float32)


def leave_kernel(own, *refs):
    parts, (residual, intersection) = refs[:-2], refs[-2:]

    def exchange(rows):
        return -FRACTION * sum(part[rows, :] for part in parts)

    mean = exchange(slice(ROWS, ROWS + 1)) * (1.0 / CELLS)
    intersection[...] = mean[:, :1]
    whole = ROWS // 8 * 8
    for row in range(0, whole, 8):
        rows = slice(row, row + 8)
        value = exchange(rows) - mean * own[rows, :]
        residual[:, row * LANES : (row + 8) * LANES] = value.reshape(1, 8 * LANES)
    rows = slice(whole, ROWS)
    residual[:, whole * LANES :] = exchange(rows) - mean * own[rows, :]


VMEM = pl.BlockSpec(memory_space=pltpu.VMEM)
SMEM = pl.BlockSpec(memory_space=pltpu.SMEM)
PARAMS = pltpu.CompilerParams(vmem_limit_bytes=8 * 1024 * 1024)


def chunks_of(count, parts):
    rows = count * PAIR_ROWS
    if parts == 1:
        return [jax.ShapeDtypeStruct((DEVICES, rows, LANES), jnp.float32)]
    return [jax.ShapeDtypeStruct((rows, LANES), jnp.float32)] * parts


def work_of(count):
    return [pltpu.VMEM((count * LINES, LANES), jnp.float32)]


def spread_pairs(orbitals, pairs, tables, parts=DEVICES):
    return pl.pallas_call(
        lambda *refs: spread_kernel(pairs, list(orbitals), *refs),
        out_shape=chunks_of(len(pairs), parts),
        in_specs=[SMEM] + [VMEM] * (len(orbitals) + 2),
        out_specs=[VMEM] * parts,
        scratch_shapes=work_of(len(pairs)),
        compiler_params=PARAMS,
        name="spread",
    )(tables["place"], *orbitals.values(), tables["lines"], tables["columns"])


def solve_pencils(chunks, count, tables):
    parts = len(chunks)
    return pl.pallas_call(
        lambda *refs: pencil_kernel(count, parts, *refs),
        out_shape=chunks_of(count, DEVICES),
        in_specs=[SMEM] + [VMEM] * (parts + 3),
        out_specs=[VMEM] * DEVICES,
        compiler_params=PARAMS,
        name="pencils",
    )(tables["place"], *chunks, tables["kernel"], tables["forward"], tables["backward"])


def gather_shares(chunks, count, orbitals, shares, tables, added=()):
    parts = len(chunks)
    return pl.pallas_call(
        lambda *refs: gather_kernel(count, parts, list(orbitals), shares, *refs),
        out_shape=[jax.ShapeDtypeStruct((PAD_ROWS, LANES), jnp.float32)] * len(shares),
        in_specs=[SMEM] + [VMEM] * (parts + 2 + len(orbitals) + len(added)),
        out_specs=[VMEM] * len(shares),
        scratch_shapes=work_of(count),
        compiler_params=PARAMS,
        name="gather",
    )(tables["place"], *chunks, tables["lines"], tables["columns"], *orbitals.values(), *added)


def enter(cells):
    return pl.pallas_call(
        enter_kernel,
        out_shape=jax.ShapeDtypeStruct((PAD_ROWS, LANES), jnp.float32),
        in_specs=[VMEM],
        out_specs=VMEM,
        compiler_params=PARAMS,
        name="enter",
    )(cells)


def leave(own, *parts):
    return pl.pallas_call(
        leave_kernel,
        out_shape=[jax.ShapeDtypeStruct((1, ROWS * LANES), jnp.float32), jax.ShapeDtypeStruct((1, 1), jnp.float32)],
        in_specs=[VMEM] * (1 + len(parts)),
        out_specs=[VMEM] * 2,
        compiler_params=PARAMS,
        name="leave",
    )(own, *parts)


def exchanged(chunks):
    if len(chunks) == 1:
        return [lax.all_to_all(chunks[0], "grid", split_axis=0, concat_axis=0)]
    received = [chunks[0]]
    for chunk, step in zip(chunks[1:], STEPS[1:]):
        pairs = [(device, device ^ step) for device in range(DEVICES)]
        received.append(lax.ppermute(chunk, "grid", pairs))
    return received


def after(values, *others):
    return lax.optimization_barrier((values, others))[0]


def swapped(value, step, phase):
    count = lax.axis_size("orb")
    pairs = []
    for source in range(count):
        upward = source // step % 2 == phase
        pairs.append((source, (source + (step if upward else -step)) % count))
    return lax.ppermute(value, "orb", pairs)


def shards(orbitals):
    device = lax.axis_index("grid")
    block = lax.axis_index("orb")
    tables = {
        "place": jnp.stack([block % 2, device]).astype(jnp.int32),
        "kernel": screened(device),
        "lines": jnp.asarray(line_weights()),
        "columns": jnp.asarray(column_weights()),
        "forward": jnp.asarray(np.stack([forward_weights(d) for d in range(DEVICES)])),
        "backward": jnp.asarray(np.stack([backward_weights(d) for d in range(DEVICES)])),
    }
    own = enter(orbitals)
    second = swapped(own, 1, 1)
    first = swapped(own, 1, 0)
    third = swapped(first, 1, 1)
    fourth = swapped(second, 1, 0)
    close = {0: own, (1, 0): first, (1, 1): second}
    near = spread_pairs(close, [(0, 1), (-1, 1)], tables)
    third, fourth = after((third, fourth), near)
    wide = {(1, 1): second, (1, 0): first, (2, 1): fourth, (2, 0): third}
    far = spread_pairs(wide, [(-1, 2), (-2, 2)], tables)
    none = spread_pairs({0: after(own, far)}, [(0, 0)], tables)
    near = solve_pencils(exchanged(near), 2, tables)
    far = solve_pencils(after(exchanged(far), near, none), 2, tables)
    near = exchanged(near)
    far = exchanged(far)
    shares = {1: [(0, 0), (1, -1)], -1: [(1, 1)], 0: [(0, 1)]}
    three, four, kept = gather_shares(near, 2, close, shares, tables)
    none = exchanged(after(none, kept))
    far = after(far, kept)
    shares = {1: [(0, -1), (1, -2)], -1: [(1, 2)], 2: [], -2: [(0, 2)]}
    one, two, three, four = gather_shares(far, 2, wide, shares, tables, [three, four])
    one = swapped(after(one, none), 1, 0)
    two = swapped(two, 1, 1)
    none = solve_pencils(none, 1, tables)
    none = exchanged(after(none, one))
    four = swapped(one + four, 1, 1)
    three = swapped(two + after(three, none), 1, 0)
    kept = kept + four
    (self_share,) = gather_shares(none, 1, {0: own}, {0: [(0, 0)]}, tables)
    residual, intersection = leave(own, self_share, kept, three)
    return residual, intersection.reshape(1, 1, 1)


def solution(mesh):
    in_specs = (P("orb", "grid"),)
    out_specs = (P("orb", "grid"), P("orb", None, None))
    return jax.shard_map(shards, mesh=mesh, in_specs=in_specs, out_specs=out_specs, check_vma=False)
```
